256 devices in a mesh: zslab: 8 (over y, x_lo), tile: 32 (over x_hi, z, core).
Axes of the slice: x: 4 (x_hi: 2, x_lo: 2; x = x_hi * 2 + x_lo), y: 4, z: 8, core: 2. Of those that a mesh axis runs over, the one named last changes fastest.
Arguments:
- estimate: float32 [128, 1024, 128], P('zslab', 'tile'), may hold values from 0.5 to 1.5
- view_data: float32 [6, 128, 1024, 128], P(None, 'zslab', 'tile'), may hold values from 0.2 to 3
- psf: float32 [6, 3, 31], replicated, may hold values from 0.05 to 1
- shifts: int32 [6], replicated, may hold values from -16 to 16, as said below
- extents: int32 [6, 2], replicated, may hold values from 0 to 128, as said below
Outputs:
- restored: float32 [128, 1024, 128], P('zslab', 'tile')
The draws below stay inside these ranges and needn't reach their ends.
Inputs may be any that keep to these rules, and one draw needn't show every extreme that they name: `shifts`: each view's x-offset lies within 16 cells; some view is offset by exactly 16 and some by exactly -16. extents[v, 0] < extents[v, 1]; every z-plane lies in the extent of at least one view.
All inputs are finite; a program needn't handle non-finite values.
Results may differ from the reference program's by a relative error of at most 0.0003.
Values sent between devices are 32-bit elements; how exact they have to be, the bound alone decides.
A program may use at most 64 MiB of HBM per device.

```python
import math
import jax
import jax.numpy as jnp
from jax import lax

V = 6
TAPS = 31
ITERS = 2
SMAX = 16
NY = 128
NZ = 128
NX = 1024


def draw_shifts(key, part):
    key = jax.random.fold_in(key, 11)
    values = jax.random.randint(key, (V,), -SMAX, SMAX + 1, dtype=jnp.int32)
    index = jnp.arange(V, dtype=jnp.int32)
    values = jnp.where(index == 0, SMAX, values)
    values = jnp.where(index == 1, -SMAX, values)
    return values.astype(jnp.int32)


def draw_extents(key, part):
    key = jax.random.fold_in(key, 23)
    first_key, second_key = jax.random.split(key)
    lower = jax.random.randint(first_key, (V,), 0, NZ // 2, dtype=jnp.int32)
    span = jax.random.randint(second_key, (V,), NZ // 4, NZ // 2 + 1, dtype=jnp.int32)
    upper = lower + span
    index = jnp.arange(V, dtype=jnp.int32)
    lower = jnp.where(index == 0, 0, lower)
    upper = jnp.where(index == 0, NZ, upper)
    return jnp.stack([lower, upper], axis=1).astype(jnp.int32)


def levels(own_key, shape, cuts, low, top_value):
    gain = 1.0
    for position, shards_of in cuts:
        heights = jax.random.uniform(jax.random.fold_in(jax.random.fold_in(own_key, 6), position), (shards_of,), jnp.float32, low / len(cuts), top_value / len(cuts))
        gain = gain * jnp.repeat(jnp.exp(heights), shape[position] // shards_of).reshape((-1,) + (1,) * (len(shape) - 1 - position))
    return gain


def setup_inputs(seed: int = 0) -> dict:
    key_of = jax.random.split(jax.random.key(seed), 6)
    return {
        "estimate": jnp.clip(0.5 + 1.0 * jax.random.uniform(key_of[0], (NZ, NX, NY), jnp.float32) ** levels(key_of[0], (NZ, NX, NY), ((0, 8), (1, 32)), -0.2, 0.2), 0.5, 1.5),
        "view_data": jnp.clip(0.2 + 2.8 * jax.random.uniform(key_of[1], (V, NZ, NX, NY), jnp.float32) ** levels(key_of[1], (V, NZ, NX, NY), ((1, 8), (2, 32)), -0.2, 0.2), 0.2, 3.0),
        "psf": jnp.clip(jnp.exp(jax.random.uniform(key_of[2], (V, 3, TAPS), jnp.float32, math.log(0.05), math.log(1.0))), 0.05, 1.0),
        "shifts": draw_shifts(jax.random.fold_in(key_of[5], 71), 0),
        "extents": draw_extents(jax.random.fold_in(key_of[5], 71), 0),
    }


def convolve(padded, kern, axis, flip, length):
    taps = kern.shape[0]
    half = taps // 2
    total = None
    for j in range(taps):
        start = 2 * half - j if flip else j
        piece = lax.slice_in_dim(padded, start, start + length, axis=axis)
        term = kern[j] * piece
        total = term if total is None else total + term
    return total


def pad_axis(volume, axis, width):
    widths = [(0, 0)] * volume.ndim
    widths[axis] = (width, width)
    return jnp.pad(volume, widths)


def blur(volume, kern, flip):
    half = kern.shape[1] // 2
    depth, rows, cols = volume.shape
    out = convolve(pad_axis(volume, 1, half), kern[0], 1, flip, rows)
    out = convolve(pad_axis(out, 2, half), kern[1], 2, flip, cols)
    out = convolve(pad_axis(out, 0, half), kern[2], 0, flip, depth)
    return out


def reference(estimate, view_data, psf, shifts, extents):
    kernels = psf / jnp.sum(psf, axis=2, keepdims=True)
    zpos = jnp.arange(NZ, dtype=jnp.int32)
    inside = ((zpos[None, :] >= extents[:, 0:1]) & (zpos[None, :] < extents[:, 1:2])).astype(jnp.float32)
    count = jnp.sum(inside, axis=0)[:, None, None]
    for step_index in range(ITERS):
        current = estimate

        def one_view(total, item):
            kern, view, shift, inner = item
            padded = jnp.pad(view, ((0, 0), (SMAX, SMAX), (0, 0)))
            data = lax.dynamic_slice_in_dim(padded, (SMAX + shift).astype(jnp.int32), NX, axis=1)
            blurred = blur(current, kern, False)
            ratio = inner[:, None, None] * data / blurred
            return total + blur(ratio, kern, True), None

        start_total = jnp.zeros(current.shape, jnp.float32)
        total, unused = lax.scan(one_view, start_total, (kernels, view_data, shifts, inside))
        estimate = current * total / count
    return estimate
```

```python
import functools

import jax
import jax.numpy as jnp
from jax import lax
from jax.experimental import pallas as pl
from jax.experimental.pallas import tpu as pltpu
from jax.sharding import PartitionSpec as P

MESH = pl.DeviceIdType.MESH
V, TAPS, ITERS = 6, 31, 2
H = TAPS // 2
W = 16
D, R, C = 16, 32, 128
DE, RE = D + 2 * W, R + 2 * W
F32, BF16 = jnp.float32, jnp.bfloat16


def halves(x):
    hi = x.astype(BF16)
    return hi, (x - hi.astype(F32)).astype(BF16)


def stacked(x):
    hi, lo = halves(x)
    return jnp.concatenate([hi, lo, hi], axis=0)


def dot(a, b):
    return jnp.dot(a, b, preferred_element_type=F32)


def band(psf, v, a, offset):
    def tap(t, carry):
        total, weight = carry
        p = psf[v, a, t]
        return jnp.where(offset == t, p, total), weight + p

    zeros = jnp.zeros(offset.shape, F32)
    total, weight = lax.fori_loop(0, TAPS, tap, (zeros, zeros))
    return total / weight


def iota(shape, dim):
    return lax.broadcasted_iota(jnp.int32, shape, dim)


def high_low(value, part):
    hi, lo = halves(value)
    return jnp.where(part == 2, lo.astype(F32), hi.astype(F32)).astype(BF16)


def kernel(
    nz, nt, est, view, psf, shifts, extents, out,
    raw, near, ext, zbuf, xbuf, rbuf, back, got_x, got_z,
    kz, kzt, kx, kxt, ky, kyt, send, recv, local,
):
    zs, ti = lax.axis_index("zslab"), lax.axis_index("tile")
    place = {"zslab": (zs, nz), "tile": (ti, nt)}

    def there(axis, step):
        me, count = place[axis]
        return me + step < count if step > 0 else me + step >= 0

    class Sent:
        def __init__(self, number, src, dst, axis, step):
            self.axis, self.step = axis, step
            self.copy = pltpu.make_async_remote_copy(
                src_ref=src, dst_ref=dst, send_sem=send.at[number], recv_sem=recv.at[number],
                device_id={axis: place[axis][0] + step}, device_id_type=MESH,
            )

        def start(self):
            pl.when(there(self.axis, self.step))(self.copy.start)

        def sent(self):
            pl.when(there(self.axis, self.step))(self.copy.wait_send)

        def arrived(self):
            pl.when(there(self.axis, -self.step))(self.copy.wait_recv)

    own_est = pltpu.make_async_copy(est, raw, local.at[0])
    own_est.start()
    own_view = pltpu.make_async_copy(view, near.at[:, W : W + R], local.at[1])
    own_view.start()

    ext[...] = jnp.zeros(ext.shape, F32)
    got_x[...] = jnp.zeros(got_x.shape, F32)
    got_z[...] = jnp.zeros(got_z.shape, F32)
    near[:, 0:W] = jnp.zeros((V * D, W, C), F32)
    near[:, W + R :] = jnp.zeros((V * D, W, C), F32)
    own_est.wait()
    for x in range(R):
        ext[W + x, W : W + D] = raw[pl.ds(x, D, stride=R)]

    barrier = pltpu.get_barrier_semaphore()
    beside = [(axis, step) for axis in ("zslab", "tile") for step in (-1, 1)]
    for axis, step in beside:

        @pl.when(there(axis, step))
        def _():
            pl.semaphore_signal(
                barrier, inc=1, device_id={axis: place[axis][0] + step}, device_id_type=MESH
            )

    pl.semaphore_wait(barrier, sum(there(axis, step).astype(jnp.int32) for axis, step in beside))

    own_x, own_z = slice(W, W + R), slice(W, W + D)
    planes = [own_z, slice(0, W), slice(W + D, DE)]
    views = [
        Sent(0, view.at[:, 0:W], near.at[:, W + R : RE], "tile", -1),
        Sent(1, view.at[:, R - W : R], near.at[:, 0:W], "tile", 1),
    ]
    est_z = [
        Sent(2, ext.at[own_x, own_z], ext.at[own_x, W + D : DE], "zslab", -1),
        Sent(3, ext.at[own_x, own_z], ext.at[own_x, 0:W], "zslab", 1),
    ]
    est_x = [
        [
            Sent(4 + 2 * k, ext.at[W : W + H, p], ext.at[W + R : W + R + H, p], "tile", -1),
            Sent(5 + 2 * k, ext.at[W + R - H : W + R, p], ext.at[1 : 1 + H, p], "tile", 1),
        ]
        for k, p in enumerate(planes)
    ]
    back_x = [
        [
            Sent(10 + 2 * k, back.at[1 : 1 + H, p], got_x.at[1, :, p], "tile", -1),
            Sent(11 + 2 * k, back.at[W + R : W + R + H, p], got_x.at[0, :, p], "tile", 1),
        ]
        for k, p in enumerate(planes)
    ]
    back_z = [
        Sent(16, back.at[own_x, 0:W], got_z.at[1], "zslab", -1),
        Sent(17, back.at[own_x, W + D : DE], got_z.at[0], "zslab", 1),
    ]

    def build():
        def one(v, carry):
            row, col = iota((D, 3 * DE), 0), iota((D, 3 * DE), 1)
            part = (col >= DE).astype(jnp.int32) + (col >= 2 * DE).astype(jnp.int32)
            kz[pl.ds(pl.multiple_of(v * D, D), D)] = high_low(
                band(psf, v, 2, col - part * DE - row - 1), part
            )
            row, col = iota((R, 3 * RE), 0), iota((R, 3 * RE), 1)
            kx[v] = high_low(band(psf, v, 0, (col & (RE - 1)) - row - 1), col // RE)
            row, col = iota((RE, 3 * R), 0), iota((RE, 3 * R), 1)
            kxt[v] = high_low(band(psf, v, 0, row - (col & (R - 1)) - 1), col // R)
            row, col = iota((C, C), 0), iota((C, C), 1)
            for mat, sign in ((ky, 1), (kyt, -1)):
                hi, lo = halves(band(psf, v, 1, sign * (row - col) + H))
                mat[v, 0:C, 0:C] = hi
                mat[v, 0:C, C:] = lo
                mat[v, C:, 0:C] = hi
                mat[v, C:, C:] = jnp.zeros((C, C), BF16)
            return carry

        lax.fori_loop(0, V, one, 0)
        shape = (DE, 3 * V * D)
        row, col = iota(shape, 0), iota(shape, 1)
        part = (col >= V * D).astype(jnp.int32) + (col >= 2 * V * D).astype(jnp.int32)
        inner = col - part * V * D

        def own(v, total):
            value = band(psf, v, 2, row - (inner & (D - 1)) - 1)
            return jnp.where(inner // D == v, value, total)

        kzt[...] = high_low(lax.fori_loop(0, V, own, jnp.zeros(shape, F32)), part)

    def along_z(i, carry):
        x = 2 * i
        o = dot(kz[...], stacked(jnp.concatenate([ext[x], ext[x + 1]], axis=1)))
        for v in range(V):
            for k in range(2):
                at = pl.multiple_of((x + k) * D, D)
                zbuf[v, pl.ds(at, D)] = o[v * D : (v + 1) * D, k * C : (k + 1) * C]
        return carry

    def one_view(v, carry):
        for i in range(0, D, 2):
            both = [zbuf[v, pl.ds(i + k, RE, stride=D)] for k in range(2)]
            o = dot(kx[v], stacked(jnp.concatenate(both, axis=1)))
            xbuf[i * R : (i + 1) * R] = o[:, :C]
            xbuf[(i + 1) * R : (i + 2) * R] = o[:, C:]
        o = dot(jnp.concatenate(halves(xbuf[...]), axis=1), ky[v])
        blurred = o[:, :C] + o[:, C:]
        start = W + shifts[v]
        for z in range(D):
            plane = zs * D + z
            inside = jnp.where((plane >= extents[v, 0]) & (plane < extents[v, 1]), 1.0, 0.0)
            data = near[v * D + z, pl.ds(start, R)]
            xbuf[z * R : (z + 1) * R] = inside * data / blurred[z * R : (z + 1) * R]
        o = dot(jnp.concatenate(halves(xbuf[...]), axis=1), kyt[v])
        xbuf[...] = o[:, :C] + o[:, C:]
        for i in range(0, D, 2):
            both = [xbuf[(i + k) * R : (i + k + 1) * R] for k in range(2)]
            o = dot(kxt[v], stacked(jnp.concatenate(both, axis=1)))
            for k in range(2):
                rbuf[pl.ds(v * D + i + k, RE, stride=V * D)] = o[:, k * C : (k + 1) * C]
        return carry

    def along_z_back(i, carry):
        x = 2 * i
        both = [rbuf[pl.ds(pl.multiple_of((x + k) * V * D, V * D), V * D)] for k in range(2)]
        o = dot(kzt[...], stacked(jnp.concatenate(both, axis=1)))
        back[x] = o[:, :C]
        back[x + 1] = o[:, C:]
        return carry

    depth = zs * D + iota((D, C), 0)
    count = jnp.zeros((D, C), F32)
    for v in range(V):
        held = (depth >= extents[v, 0]) & (depth < extents[v, 1])
        count = count + jnp.where(held, 1.0, 0.0)

    for step in range(ITERS):
        for copy in est_z + est_x[0]:
            copy.start()
        if step == 0:
            for copy in views:
                copy.start()
            build()
        est_z[0].arrived()
        for copy in est_x[2]:
            copy.start()
        est_z[1].arrived()
        for copy in est_x[1]:
            copy.start()
        for pair in est_x:
            for copy in pair:
                copy.arrived()
        lax.fori_loop(0, RE // 2, along_z, 0, unroll=2)
        if step == 0:
            own_view.wait()
            for copy in views:
                copy.arrived()
        lax.fori_loop(0, V, one_view, 0)
        lax.fori_loop(0, RE // 2, along_z_back, 0, unroll=2)
        for pair in (back_x[1], back_x[2], back_x[0]):
            for copy in pair:
                copy.start()
        for copy in est_z:
            copy.sent()
        for pair in est_x:
            for copy in pair:
                copy.sent()
        for k in (1, 2, 0):
            for copy in back_x[k]:
                copy.arrived()
            p = planes[k]
            back[W : W + H, p] += got_x[0, :, p]
            back[W + R - H : W + R, p] += got_x[1, :, p]
            if k > 0:
                back_z[k - 1].start()
        for copy in back_z:
            copy.arrived()
        for x in range(R):
            total = back[W + x, own_z] + got_z[0, x] + got_z[1, x]
            updated = ext[W + x, own_z] * total / count
            if step < ITERS - 1:
                ext[W + x, own_z] = updated
            else:
                out[pl.ds(x, D, stride=R)] = updated
        for pair in back_x + [back_z]:
            for copy in pair:
                copy.sent()
    for copy in views:
        copy.sent()


def solution(mesh):
    nz, nt = mesh.shape["zslab"], mesh.shape["tile"]

    def per_device(estimate, view_data, psf, shifts, extents):
        flat = pl.pallas_call(
            functools.partial(kernel, nz, nt),
            out_shape=jax.ShapeDtypeStruct((D * R, C), F32),
            in_specs=[pl.BlockSpec(memory_space=pl.ANY)] * 2
            + [pl.BlockSpec(memory_space=pltpu.SMEM)] * 3,
            out_specs=pl.BlockSpec(memory_space=pltpu.VMEM),
            scratch_shapes=[
                pltpu.VMEM((D * R, C), F32),
                pltpu.VMEM((V * D, RE, C), F32),
                pltpu.VMEM((RE, DE, C), F32),
                pltpu.VMEM((V, RE * D, C), F32),
                pltpu.VMEM((D * R, C), F32),
                pltpu.VMEM((RE * V * D, C), F32),
                pltpu.VMEM((RE, DE, C), F32),
                pltpu.VMEM((2, H, DE, C), F32),
                pltpu.VMEM((2, R, D, C), F32),
                pltpu.VMEM((V * D, 3 * DE), BF16),
                pltpu.VMEM((DE, 3 * V * D), BF16),
                pltpu.VMEM((V, R, 3 * RE), BF16),
                pltpu.VMEM((V, RE, 3 * R), BF16),
                pltpu.VMEM((V, 2 * C, 2 * C), BF16),
                pltpu.VMEM((V, 2 * C, 2 * C), BF16),
                pltpu.SemaphoreType.DMA((18,)),
                pltpu.SemaphoreType.DMA((18,)),
                pltpu.SemaphoreType.DMA((2,)),
            ],
            compiler_params=pltpu.CompilerParams(
                collective_id=0, has_side_effects=True, vmem_limit_bytes=48 * 1024 * 1024
            ),
        )(
            estimate.reshape(D * R, C),
            view_data.reshape(V * D, R, C),
            psf,
            shifts,
            extents,
        )
        return flat.reshape(D, R, C)

    placed = (P("zslab", "tile", None), P(None, "zslab", "tile", None), P(), P(), P())
    return jax.shard_map(
        per_device, mesh=mesh, in_specs=placed, out_specs=P("zslab", "tile", None), check_vma=False
    )
```

```python
import functools

import jax
import jax.numpy as jnp
from jax import lax
from jax.experimental import pallas as pl
from jax.experimental.pallas import tpu as pltpu
from jax.sharding import PartitionSpec as P

MESH = pl.DeviceIdType.MESH
V, TAPS, ITERS = 6, 31, 2
H = TAPS // 2
W = 16
D, R, C = 16, 32, 128
DE, RE = D + 2 * W, R + 2 * W
N = 8
ORDER = (0, 24, 8, 16)
SEMS = 2 + 10 * len(ORDER)
F32, BF16 = jnp.float32, jnp.bfloat16


def halves(x):
    hi = x.astype(BF16)
    return hi, (x - hi.astype(F32)).astype(BF16)


def stacked(x):
    hi, lo = halves(x)
    return jnp.concatenate([hi, lo, hi], axis=0)


def dot(a, b):
    return jnp.dot(a, b, preferred_element_type=F32)


def split_part(value):
    hi, lo = halves(value)
    return hi.astype(F32), lo.astype(F32)


def iota(shape, dim):
    return lax.broadcasted_iota(jnp.int32, shape, dim)


def taps(psf, v, a):
    lane = iota((8, C), 1)
    forward = jnp.zeros((8, C), F32)
    reverse = jnp.zeros((8, C), F32)
    for t in range(TAPS):
        p = psf[v, a, t]
        forward = jnp.where(lane == t, p, forward)
        reverse = jnp.where(lane == TAPS - 1 - t, p, reverse)
    weight = jnp.sum(forward, axis=1, keepdims=True)
    return forward / weight, reverse / weight


def slanted(row, rows, first):
    whole = jnp.concatenate([row] * (rows // 8), axis=0)
    return pltpu.roll(whole, first % C, 1, stride=1, stride_axis=0)


def kernel(
    nz, nt, est, view, psf_in, shifts_in, extents_in, out,
    raw, near, ext, zbuf, xbuf, rbuf, back, got_x, got_y, got_n,
    kz, kzt, kx, kxt, ky, kyt, psf, shifts, extents, send, recv, local,
):
    zs, ti = lax.axis_index("zslab"), lax.axis_index("tile")
    odd = lax.rem(zs, 2)
    mate, ahead, behind = zs + 1 - 2 * odd, zs + 2 - 4 * odd, zs - 2 + 4 * odd
    close = pl.multiple_of(2 * W * (1 - odd), W)
    far = pl.multiple_of(2 * W * odd, W)
    is_mate = mate < nz

    class Sent:
        def __init__(self, number, src, dst, axis, target, exists, comes):
            self.exists, self.comes = exists, comes
            self.copy = pltpu.make_async_remote_copy(
                src_ref=src, dst_ref=dst, send_sem=send.at[number], recv_sem=recv.at[number],
                device_id={axis: target}, device_id_type=MESH,
            )

        def start(self):
            pl.when(self.exists)(self.copy.start)

        def sent(self):
            pl.when(self.exists)(self.copy.wait_send)

        def arrived(self):
            pl.when(self.comes)(self.copy.wait_recv)

    is_ahead = (ahead >= 0) & (ahead < nz)
    is_behind = (behind >= 0) & (behind < nz)
    is_left, is_right = ti > 0, ti < nt - 1
    numbers = iter(range(SEMS))

    def to_mate(src, dst):
        return Sent(next(numbers), src, dst, "zslab", mate, is_mate, is_mate)

    def to_ahead(src, dst):
        return Sent(next(numbers), src, dst, "zslab", ahead, is_ahead, is_behind)

    def to_behind(src, dst):
        return Sent(next(numbers), src, dst, "zslab", behind, is_behind, is_ahead)

    def to_left(src, dst):
        return Sent(next(numbers), src, dst, "tile", ti - 1, is_left, is_right)

    def to_right(src, dst):
        return Sent(next(numbers), src, dst, "tile", ti + 1, is_right, is_left)

    reads = [
        pltpu.make_async_copy(src, dst, local.at[k])
        for k, (src, dst) in enumerate(
            [(est, raw), (view, near.at[:, W : W + R]), (psf_in, psf), (shifts_in, shifts), (extents_in, extents)]
        )
    ]
    for read in reads:
        read.start()

    ext[...] = jnp.zeros(ext.shape, F32)
    got_x[...] = jnp.zeros(got_x.shape, F32)
    got_y[...] = jnp.zeros(got_y.shape, F32)
    near[:, 0:W] = jnp.zeros((V * D, W, C), F32)
    near[:, W + R :] = jnp.zeros((V * D, W, C), F32)
    for x in range(RE):
        rbuf[pl.ds(x * C + V * D, C - V * D)] = jnp.zeros((C - V * D, C), F32)
    reads[0].wait()
    for x in range(R):
        ext[W + x, W : W + D] = raw[pl.ds(x, D, stride=R)]

    barrier = pltpu.get_barrier_semaphore()
    beside = [
        ("zslab", mate, is_mate), ("zslab", ahead, is_ahead), ("zslab", behind, is_behind),
        ("tile", ti - 1, is_left), ("tile", ti + 1, is_right),
    ]
    for axis, target, exists in beside:

        @pl.when(exists)
        def _(axis=axis, target=target):
            pl.semaphore_signal(barrier, inc=1, device_id={axis: target}, device_id_type=MESH)

    pl.semaphore_wait(barrier, sum(exists.astype(jnp.int32) for _, _, exists in beside))

    own_p, close_p, far_p = pl.ds(W, D), pl.ds(close, W), pl.ds(far, W)

    def rows_of(r):
        return slice(W + r, W + r + N)

    def est_tile(r, p):
        src = ext.at[rows_of(r), p]
        if r < W:
            return to_left(src, ext.at[W + R + r : W + R + r + N, p])
        return to_right(src, ext.at[r - W : r - W + N, p])

    def back_tile(r, p):
        dst = got_x.at[r : r + N, p]
        if r < W:
            return to_right(back.at[W + R + r : W + R + r + N, p], dst)
        return to_left(back.at[r - W : r - W + N, p], dst)

    views = [
        to_left(view.at[:, 0:W], near.at[:, W + R : RE]),
        to_right(view.at[:, R - W : R], near.at[:, 0:W]),
    ]
    est_mate = {r: to_mate(ext.at[rows_of(r), own_p], ext.at[rows_of(r), far_p]) for r in ORDER}
    est_ahead = {r: to_ahead(ext.at[rows_of(r), close_p], ext.at[rows_of(r), far_p]) for r in ORDER}
    est_own = {r: est_tile(r, own_p) for r in ORDER}
    est_close = {r: est_tile(r, close_p) for r in ORDER}
    est_far = {r: est_tile(r, far_p) for r in ORDER}
    back_far = {r: back_tile(r, far_p) for r in ORDER}
    back_close = {r: back_tile(r, close_p) for r in ORDER}
    back_own = {r: back_tile(r, own_p) for r in ORDER}
    back_behind = {r: to_behind(back.at[rows_of(r), far_p], got_y.at[r : r + N]) for r in ORDER}
    back_mate = {r: to_mate(back.at[rows_of(r), close_p], got_n.at[r : r + N]) for r in ORDER}
    est_sends = [est_mate, est_ahead, est_own, est_close, est_far]
    back_sends = [back_far, back_close, back_own, back_behind, back_mate]

    def build():
        lane = iota((C, C), 1)
        gap = iota((C, C), 0) - lane
        banded = (gap >= -H) & (gap <= H)

        def one(v, total):
            forward, reverse = taps(psf, v, 2)
            hi, lo = split_part(slanted(forward, D, 1))
            low = pltpu.roll(lo, 2 * DE, 1)
            at = pl.ds(pl.multiple_of(v * D, D), D)
            kz[at, 0:C] = (
                hi + pltpu.roll(hi, DE, 1) + jnp.where(lane[0:D] >= 2 * DE, low, 0.0)
            ).astype(BF16)
            kz[at, C:] = low[:, 0 : 3 * DE - C].astype(BF16)
            z_back = jnp.where(lane[0:DE] < D, slanted(reverse, DE, -TAPS), 0.0)
            forward, reverse = taps(psf, v, 0)
            hi, lo = split_part(slanted(forward, R, 1))
            kx[v, :, 0:C] = (hi + pltpu.roll(hi, RE, 1)).astype(BF16)
            kx[v, :, C:] = lo[:, 0:RE].astype(BF16)
            hi, lo = split_part(jnp.where(lane[0:RE] < R, slanted(reverse, RE, -TAPS), 0.0))
            kxt[v] = (hi + pltpu.roll(hi, R, 1) + pltpu.roll(lo, 2 * R, 1))[:, 0 : 3 * R].astype(BF16)
            forward, reverse = taps(psf, v, 1)
            for mat, row in ((ky, reverse), (kyt, forward)):
                hi, lo = halves(jnp.where(banded, slanted(row, C, -H), 0.0))
                mat[v, 0:C, 0:C] = hi
                mat[v, 0:C, C:] = lo
                mat[v, C:, 0:C] = hi
                mat[v, C:, C:] = jnp.zeros((C, C), BF16)
            return total + pltpu.roll(z_back, v * D, 1)

        hi, lo = halves(lax.fori_loop(0, V, one, jnp.zeros((DE, C), F32)))
        kzt[:, 0:C] = hi
        kzt[:, C : 2 * C] = hi
        kzt[:, 2 * C :] = lo

    def along_z(i, carry):
        x = 2 * i
        o = dot(kz[...], stacked(jnp.concatenate([ext[x], ext[x + 1]], axis=1)))
        for v in range(V):
            for k in range(2):
                at = pl.multiple_of((x + k) * D, D)
                zbuf[v, pl.ds(at, D)] = o[v * D : (v + 1) * D, k * C : (k + 1) * C]
        return carry

    def one_view(v, carry):
        for i in range(0, D, 2):
            both = [zbuf[v, pl.ds(i + k, RE, stride=D)] for k in range(2)]
            o = dot(kx[v], stacked(jnp.concatenate(both, axis=1)))
            xbuf[i * R : (i + 1) * R] = o[:, :C]
            xbuf[(i + 1) * R : (i + 2) * R] = o[:, C:]
        o = dot(jnp.concatenate(halves(xbuf[...]), axis=1), ky[v])
        blurred = o[:, :C] + o[:, C:]
        start = W + shifts[v]
        for z in range(D):
            plane = zs * D + z
            inside = jnp.where((plane >= extents[v, 0]) & (plane < extents[v, 1]), 1.0, 0.0)
            data = near[v * D + z, pl.ds(start, R)]
            xbuf[z * R : (z + 1) * R] = inside * data / blurred[z * R : (z + 1) * R]
        o = dot(jnp.concatenate(halves(xbuf[...]), axis=1), kyt[v])
        xbuf[...] = o[:, :C] + o[:, C:]
        for i in range(0, D, 2):
            both = [xbuf[(i + k) * R : (i + k + 1) * R] for k in range(2)]
            o = dot(kxt[v], stacked(jnp.concatenate(both, axis=1)))
            for k in range(2):
                rbuf[pl.ds(v * D + i + k, RE, stride=C)] = o[:, k * C : (k + 1) * C]
        return carry

    def along_z_back(i, carry):
        x = 2 * i
        both = [rbuf[pl.ds(pl.multiple_of((x + k) * C, C), C)] for k in range(2)]
        o = dot(kzt[...], stacked(jnp.concatenate(both, axis=1)))
        back[x] = o[:, :C]
        back[x + 1] = o[:, C:]
        return carry

    def over(body, first, rows):
        lax.fori_loop(first // 2, (first + rows) // 2, body, 0, unroll=2)

    for r in ORDER:
        est_mate[r].start()
        est_own[r].start()
    for copy in views:
        copy.start()
    for read in reads[2:]:
        read.wait()
    build()
    depth = zs * D + iota((D, C), 0)
    count = jnp.zeros((D, C), F32)
    for v in range(V):
        held = (depth >= extents[v, 0]) & (depth < extents[v, 1])
        count = count + jnp.where(held, 1.0, 0.0)

    for step in range(ITERS):
        for r in ORDER:
            est_mate[r].arrived()
            est_ahead[r].start()
            est_close[r].start()
        for r in ORDER:
            est_ahead[r].arrived()
            est_far[r].start()
            over(along_z, W + r, N)
        for r in ORDER:
            for group in (est_own, est_close, est_far):
                group[r].arrived()
            over(along_z, W + R + r if r < W else r - W, N)
        if step == 0:
            reads[1].wait()
            for copy in views:
                copy.arrived()
        lax.fori_loop(0, V, one_view, 0)
        for group in est_sends:
            for r in ORDER:
                group[r].sent()
        for r in ORDER:
            over(along_z_back, W + R + r if r < W else r - W, N)
            back_far[r].start()
        for group in (back_close, back_own):
            for r in ORDER:
                group[r].start()
        over(along_z_back, W, R)
        for r in ORDER:
            back_far[r].arrived()
            back[rows_of(r), far_p] += got_x[r : r + N, far_p]
            back_behind[r].start()
        for r in ORDER:
            back_close[r].arrived()
            back_behind[r].arrived()
            back[rows_of(r), close_p] += got_x[r : r + N, close_p] + got_y[r : r + N]
            back_mate[r].start()
        for r in ORDER:
            back_own[r].arrived()
            back_mate[r].arrived()
            for x in range(r, r + N):
                total = back[W + x, W : W + D] + got_x[x, W : W + D] + got_n[x]
                updated = ext[W + x, W : W + D] * total / count
                if step < ITERS - 1:
                    ext[W + x, W : W + D] = updated
                else:
                    out[pl.ds(x, D, stride=R)] = updated
            if step < ITERS - 1:
                est_mate[r].start()
                est_own[r].start()
        for group in back_sends:
            for r in ORDER:
                group[r].sent()
    for copy in views:
        copy.sent()


def solution(mesh):
    nz, nt = mesh.shape["zslab"], mesh.shape["tile"]

    def per_device(estimate, view_data, psf, shifts, extents):
        flat = pl.pallas_call(
            functools.partial(kernel, nz, nt),
            out_shape=jax.ShapeDtypeStruct((D * R, C), F32),
            in_specs=[pl.BlockSpec(memory_space=pl.ANY)] * 5,
            out_specs=pl.BlockSpec(memory_space=pltpu.VMEM),
            scratch_shapes=[
                pltpu.VMEM((D * R, C), F32),
                pltpu.VMEM((V * D, RE, C), F32),
                pltpu.VMEM((RE, DE, C), F32),
                pltpu.VMEM((V, RE * D, C), F32),
                pltpu.VMEM((D * R, C), F32),
                pltpu.VMEM((RE * C, C), F32),
                pltpu.VMEM((RE, DE, C), F32),
                pltpu.VMEM((R, DE, C), F32),
                pltpu.VMEM((R, D, C), F32),
                pltpu.VMEM((R, D, C), F32),
                pltpu.VMEM((V * D, 3 * DE), BF16),
                pltpu.VMEM((DE, 3 * C), BF16),
                pltpu.VMEM((V, R, 3 * RE), BF16),
                pltpu.VMEM((V, RE, 3 * R), BF16),
                pltpu.VMEM((V, 2 * C, 2 * C), BF16),
                pltpu.VMEM((V, 2 * C, 2 * C), BF16),
                pltpu.SMEM((V, 3, TAPS), F32),
                pltpu.SMEM((V,), jnp.int32),
                pltpu.SMEM((V, 2), jnp.int32),
                pltpu.SemaphoreType.DMA((SEMS,)),
                pltpu.SemaphoreType.DMA((SEMS,)),
                pltpu.SemaphoreType.DMA((5,)),
            ],
            compiler_params=pltpu.CompilerParams(
                collective_id=0, has_side_effects=True, vmem_limit_bytes=60 * 1024 * 1024
            ),
        )(
            estimate.reshape(D * R, C),
            view_data.reshape(V * D, R, C),
            psf,
            shifts,
            extents,
        )
        return flat.reshape(D, R, C)

    placed = (P("zslab", "tile", None), P(None, "zslab", "tile", None), P(), P(), P())
    return jax.shard_map(
        per_device, mesh=mesh, in_specs=placed, out_specs=P("zslab", "tile", None), check_vma=False
    )
```

```python
import functools

import jax
import jax.numpy as jnp
from jax import lax
from jax.experimental import pallas as pl
from jax.experimental.pallas import tpu as pltpu
from jax.sharding import PartitionSpec as P

MESH = pl.DeviceIdType.MESH
V, TAPS, ITERS = 6, 31, 2
H = TAPS // 2
W = 16
D, R, C = 16, 32, 128
DE, RE = D + 2 * W, R + 2 * W
N = 8
ORDER = (0, 24, 8, 16)
SEMS = 2 + 12 * len(ORDER)
F32, BF16 = jnp.float32, jnp.bfloat16


def halves(x):
    hi = x.astype(BF16)
    return hi, (x - hi.astype(F32)).astype(BF16)


def stacked(x):
    hi, lo = halves(x)
    return jnp.concatenate([hi, lo, hi], axis=0)


def dot(a, b):
    return jnp.dot(a, b, preferred_element_type=F32)


def split_part(value):
    hi, lo = halves(value)
    return hi.astype(F32), lo.astype(F32)


def iota(shape, dim):
    return lax.broadcasted_iota(jnp.int32, shape, dim)


def taps(psf, v, a):
    lane = iota((8, C), 1)
    forward = jnp.zeros((8, C), F32)
    reverse = jnp.zeros((8, C), F32)
    for t in range(TAPS):
        p = psf[v, a, t]
        forward = jnp.where(lane == t, p, forward)
        reverse = jnp.where(lane == TAPS - 1 - t, p, reverse)
    weight = jnp.sum(forward, axis=1, keepdims=True)
    return forward / weight, reverse / weight


def slanted(row, rows, first):
    whole = jnp.concatenate([row] * (rows // 8), axis=0)
    return pltpu.roll(whole, first % C, 1, stride=1, stride_axis=0)


def kernel(
    nz, nt, est, view, psf_in, shifts_in, extents_in, out,
    raw, near, ext, zbuf, xbuf, rbuf, back, got_x, got_y, got_n, got_h,
    kz, kzt, kx, kxt, ky, kyt, psf, shifts, extents, send, recv, local,
):
    zs, ti = lax.axis_index("zslab"), lax.axis_index("tile")
    odd = lax.rem(zs, 2)
    mate, ahead, behind = zs + 1 - 2 * odd, zs + 2 - 4 * odd, zs - 2 + 4 * odd
    close = pl.multiple_of(2 * W * (1 - odd), W)
    far = pl.multiple_of(2 * W * odd, W)
    is_mate = mate < nz

    class Sent:
        def __init__(self, number, src, dst, target, exists, comes):
            self.exists, self.comes = exists, comes
            self.copy = pltpu.make_async_remote_copy(
                src_ref=src, dst_ref=dst, send_sem=send.at[number], recv_sem=recv.at[number],
                device_id=target, device_id_type=MESH,
            )

        def start(self):
            pl.when(self.exists)(self.copy.start)

        def sent(self):
            pl.when(self.exists)(self.copy.wait_send)

        def arrived(self, where=True):
            pl.when(self.comes & where)(self.copy.wait_recv)

    is_ahead = (ahead >= 0) & (ahead < nz)
    is_behind = (behind >= 0) & (behind < nz)
    is_left, is_right = ti > 0, ti < nt - 1
    seam = nt // 2 if nz % 2 == 0 else -1
    seam_left, seam_right = is_left & (ti == seam), is_right & (ti == seam - 1)
    left = {"zslab": jnp.where(seam_left, mate, zs), "tile": ti - 1}
    right = {"zslab": jnp.where(seam_right, mate, zs), "tile": ti + 1}
    numbers = iter(range(SEMS))

    def to_mate(src, dst):
        return Sent(next(numbers), src, dst, {"zslab": mate}, is_mate, is_mate)

    def to_ahead(src, dst, where=True):
        return Sent(
            next(numbers), src, dst, {"zslab": ahead}, is_ahead & where, is_behind & where
        )

    def to_behind(src, dst, where=True):
        return Sent(
            next(numbers), src, dst, {"zslab": behind}, is_behind & where, is_ahead & where
        )

    reads = [
        pltpu.make_async_copy(src, dst, local.at[k])
        for k, (src, dst) in enumerate(
            [(est, raw), (view, near.at[:, W : W + R]), (psf_in, psf), (shifts_in, shifts), (extents_in, extents)]
        )
    ]
    for read in reads:
        read.start()

    ext[...] = jnp.zeros(ext.shape, F32)
    got_x[...] = jnp.zeros(got_x.shape, F32)
    got_y[...] = jnp.zeros(got_y.shape, F32)
    got_h[...] = jnp.zeros(got_h.shape, F32)
    near[:, 0:W] = jnp.zeros((V * D, W, C), F32)
    near[:, W + R :] = jnp.zeros((V * D, W, C), F32)
    for x in range(RE):
        rbuf[pl.ds(x * C + V * D, C - V * D)] = jnp.zeros((C - V * D, C), F32)
    reads[0].wait()
    for x in range(R):
        ext[W + x, W : W + D] = raw[pl.ds(x, D, stride=R)]

    barrier = pltpu.get_barrier_semaphore()
    beside = [
        ({"zslab": mate}, is_mate), ({"zslab": ahead}, is_ahead), ({"zslab": behind}, is_behind),
        ({"tile": ti - 1}, is_left), ({"tile": ti + 1}, is_right),
        (left, seam_left), (right, seam_right),
    ]
    for target, exists in beside:

        @pl.when(exists)
        def _(target=target):
            pl.semaphore_signal(barrier, inc=1, device_id=target, device_id_type=MESH)

    pl.semaphore_wait(barrier, sum(exists.astype(jnp.int32) for _, exists in beside))

    own_p, close_p, far_p = pl.ds(W, D), pl.ds(close, W), pl.ds(far, W)

    def rows_of(r):
        return slice(W + r, W + r + N)

    def beyond(r):
        return slice(W + R + r, W + R + r + N) if r < W else slice(r - W, r - W + N)

    def crossed(where, p):
        if p is far_p:
            return p
        start, other = (W, far) if p is own_p else (close, W)
        return pl.ds(pl.multiple_of(jnp.where(where, other, start), W), W)

    def to_tile(leftward, src, dst, p):
        seam_out, seam_in = (seam_left, seam_right) if leftward else (seam_right, seam_left)
        exists, comes = (is_left, is_right) if leftward else (is_right, is_left)
        if p is far_p:
            exists, comes = exists & jnp.logical_not(seam_out), comes & jnp.logical_not(seam_in)
        return Sent(
            next(numbers), src, dst.at[:, crossed(seam_out, p)], left if leftward else right, exists, comes
        )

    def est_tile(r, p):
        return to_tile(r < W, ext.at[rows_of(r), p], ext.at[beyond(r)], p)

    def back_tile(r, p):
        return to_tile(r >= W, back.at[beyond(r), p], got_x.at[r : r + N], p)

    def at_seam(r):
        return seam_right if r < W else seam_left

    def by_seam(r):
        return seam_left if r < W else seam_right

    views = [
        Sent(next(numbers), view.at[:, 0:W], near.at[:, W + R : RE], {"tile": ti - 1}, is_left, is_right),
        Sent(next(numbers), view.at[:, R - W : R], near.at[:, 0:W], {"tile": ti + 1}, is_right, is_left),
    ]
    est_mate = {r: to_mate(ext.at[rows_of(r), own_p], ext.at[rows_of(r), far_p]) for r in ORDER}
    est_ahead = {r: to_ahead(ext.at[rows_of(r), close_p], ext.at[rows_of(r), far_p]) for r in ORDER}
    est_halo = {
        r: to_ahead(ext.at[beyond(r), close_p], ext.at[beyond(r), far_p], at_seam(r)) for r in ORDER
    }
    est_own = {r: est_tile(r, own_p) for r in ORDER}
    est_close = {r: est_tile(r, close_p) for r in ORDER}
    est_far = {r: est_tile(r, far_p) for r in ORDER}
    back_halo = {r: to_behind(back.at[beyond(r), far_p], got_h.at[r : r + N], at_seam(r)) for r in ORDER}
    back_far = {r: back_tile(r, far_p) for r in ORDER}
    back_close = {r: back_tile(r, close_p) for r in ORDER}
    back_own = {r: back_tile(r, own_p) for r in ORDER}
    back_behind = {r: to_behind(back.at[rows_of(r), far_p], got_y.at[r : r + N]) for r in ORDER}
    back_mate = {r: to_mate(back.at[rows_of(r), close_p], got_n.at[r : r + N]) for r in ORDER}
    est_sends = [est_mate, est_ahead, est_halo, est_own, est_close, est_far]
    back_sends = [back_halo, back_far, back_close, back_own, back_behind, back_mate]

    def build():
        lane = iota((C, C), 1)
        gap = iota((C, C), 0) - lane
        banded = (gap >= -H) & (gap <= H)

        def one(v, total):
            forward, reverse = taps(psf, v, 2)
            hi, lo = split_part(slanted(forward, D, 1))
            low = pltpu.roll(lo, 2 * DE, 1)
            at = pl.ds(pl.multiple_of(v * D, D), D)
            kz[at, 0:C] = (
                hi + pltpu.roll(hi, DE, 1) + jnp.where(lane[0:D] >= 2 * DE, low, 0.0)
            ).astype(BF16)
            kz[at, C:] = low[:, 0 : 3 * DE - C].astype(BF16)
            z_back = jnp.where(lane[0:DE] < D, slanted(reverse, DE, -TAPS), 0.0)
            forward, reverse = taps(psf, v, 0)
            hi, lo = split_part(slanted(forward, R, 1))
            kx[v, :, 0:C] = (hi + pltpu.roll(hi, RE, 1)).astype(BF16)
            kx[v, :, C:] = lo[:, 0:RE].astype(BF16)
            hi, lo = split_part(jnp.where(lane[0:RE] < R, slanted(reverse, RE, -TAPS), 0.0))
            kxt[v] = (hi + pltpu.roll(hi, R, 1) + pltpu.roll(lo, 2 * R, 1))[:, 0 : 3 * R].astype(BF16)
            forward, reverse = taps(psf, v, 1)
            for mat, row in ((ky, reverse), (kyt, forward)):
                hi, lo = halves(jnp.where(banded, slanted(row, C, -H), 0.0))
                mat[v, 0:C, 0:C] = hi
                mat[v, 0:C, C:] = lo
                mat[v, C:, 0:C] = hi
                mat[v, C:, C:] = jnp.zeros((C, C), BF16)
            return total + pltpu.roll(z_back, v * D, 1)

        hi, lo = halves(lax.fori_loop(0, V, one, jnp.zeros((DE, C), F32)))
        kzt[:, 0:C] = hi
        kzt[:, C : 2 * C] = hi
        kzt[:, 2 * C :] = lo

    def along_z(i, carry):
        x = 2 * i
        o = dot(kz[...], stacked(jnp.concatenate([ext[x], ext[x + 1]], axis=1)))
        for v in range(V):
            for k in range(2):
                at = pl.multiple_of((x + k) * D, D)
                zbuf[v, pl.ds(at, D)] = o[v * D : (v + 1) * D, k * C : (k + 1) * C]
        return carry

    def one_view(v, carry):
        for i in range(0, D, 2):
            both = [zbuf[v, pl.ds(i + k, RE, stride=D)] for k in range(2)]
            o = dot(kx[v], stacked(jnp.concatenate(both, axis=1)))
            xbuf[i * R : (i + 1) * R] = o[:, :C]
            xbuf[(i + 1) * R : (i + 2) * R] = o[:, C:]
        o = dot(jnp.concatenate(halves(xbuf[...]), axis=1), ky[v])
        blurred = o[:, :C] + o[:, C:]
        start = W + shifts[v]
        for z in range(D):
            plane = zs * D + z
            inside = jnp.where((plane >= extents[0, v]) & (plane < extents[1, v]), 1.0, 0.0)
            data = near[v * D + z, pl.ds(start, R)]
            xbuf[z * R : (z + 1) * R] = inside * data / blurred[z * R : (z + 1) * R]
        o = dot(jnp.concatenate(halves(xbuf[...]), axis=1), kyt[v])
        xbuf[...] = o[:, :C] + o[:, C:]
        for i in range(0, D, 2):
            both = [xbuf[(i + k) * R : (i + k + 1) * R] for k in range(2)]
            o = dot(kxt[v], stacked(jnp.concatenate(both, axis=1)))
            for k in range(2):
                rbuf[pl.ds(v * D + i + k, RE, stride=C)] = o[:, k * C : (k + 1) * C]
        return carry

    def along_z_back(i, carry):
        x = 2 * i
        both = [rbuf[pl.ds(pl.multiple_of((x + k) * C, C), C)] for k in range(2)]
        o = dot(kzt[...], stacked(jnp.concatenate(both, axis=1)))
        back[x] = o[:, :C]
        back[x + 1] = o[:, C:]
        return carry

    def over(body, first, rows):
        lax.fori_loop(first // 2, (first + rows) // 2, body, 0, unroll=2)

    for r in ORDER:
        est_mate[r].start()
        est_own[r].start()
    for copy, late in zip(views, (seam_left, seam_right)):
        pl.when(jnp.logical_not(late))(copy.start)
    for read in reads[2:]:
        read.wait()
    build()
    depth = zs * D + iota((D, C), 0)
    count = jnp.zeros((D, C), F32)
    for v in range(V):
        held = (depth >= extents[0, v]) & (depth < extents[1, v])
        count = count + jnp.where(held, 1.0, 0.0)

    for step in range(ITERS):
        for r in ORDER:
            est_mate[r].arrived()
            est_ahead[r].start()
            est_close[r].start()
        if step == 0:
            for copy, late in zip(views, (seam_left, seam_right)):
                pl.when(late)(copy.start)
        for r in ORDER:
            est_own[r].arrived(at_seam(r))
            est_halo[r].start()
        for r in ORDER:
            est_ahead[r].arrived()
            est_far[r].start()
            over(along_z, W + r, N)
        for r in ORDER:
            est_own[r].arrived(jnp.logical_not(at_seam(r)))
            est_close[r].arrived()
            est_far[r].arrived()
            est_halo[r].arrived()
            over(along_z, beyond(r).start, N)
        if step == 0:
            reads[1].wait()
            for copy in views:
                copy.arrived()
        lax.fori_loop(0, V, one_view, 0)
        for group in est_sends:
            for r in ORDER:
                group[r].sent()
        for r in ORDER:
            over(along_z_back, beyond(r).start, N)
            back_halo[r].start()
            back_far[r].start()
        for r in ORDER:
            pl.when(jnp.logical_not(at_seam(r)))(back_close[r].start)
        for r in ORDER:
            back_own[r].start()
        over(along_z_back, W, R)
        for r in ORDER:

            @pl.when(at_seam(r))
            def _():
                back_halo[r].arrived()
                back[beyond(r), close_p] += got_h[r : r + N]
                back_close[r].start()

        for r in ORDER:
            back_far[r].arrived()
            back[rows_of(r), far_p] += got_x[r : r + N, far_p]
            back_behind[r].start()
        for r in ORDER:
            back_close[r].arrived(jnp.logical_not(by_seam(r)))
            back_own[r].arrived(by_seam(r))
            back_behind[r].arrived()
            back[rows_of(r), close_p] += got_x[r : r + N, close_p] + got_y[r : r + N]
            back_mate[r].start()
        for r in ORDER:
            back_own[r].arrived(jnp.logical_not(by_seam(r)))
            back_close[r].arrived(by_seam(r))
            back_mate[r].arrived()
            for x in range(r, r + N):
                total = back[W + x, W : W + D] + got_x[x, W : W + D] + got_n[x]
                updated = ext[W + x, W : W + D] * total / count
                if step < ITERS - 1:
                    ext[W + x, W : W + D] = updated
                else:
                    out[pl.ds(x, D, stride=R)] = updated
            if step < ITERS - 1:
                est_mate[r].start()
                est_own[r].start()
        for group in back_sends:
            for r in ORDER:
                group[r].sent()
    for copy in views:
        copy.sent()


def solution(mesh):
    nz, nt = mesh.shape["zslab"], mesh.shape["tile"]

    def per_device(estimate, view_data, psf, shifts, extents):
        flat = pl.pallas_call(
            functools.partial(kernel, nz, nt),
            out_shape=pltpu.VMEM((D * R, C), F32),
            in_specs=[pl.BlockSpec(memory_space=pltpu.HBM)] * 5,
            out_specs=pl.BlockSpec(memory_space=pltpu.VMEM),
            scratch_shapes=[
                pltpu.VMEM((D * R, C), F32),
                pltpu.VMEM((V * D, RE, C), F32),
                pltpu.VMEM((RE, DE, C), F32),
                pltpu.VMEM((V, RE * D, C), F32),
                pltpu.VMEM((D * R, C), F32),
                pltpu.VMEM((RE * C, C), F32),
                pltpu.VMEM((RE, DE, C), F32),
                pltpu.VMEM((R, DE, C), F32),
                pltpu.VMEM((R, D, C), F32),
                pltpu.VMEM((R, D, C), F32),
                pltpu.VMEM((R, D, C), F32),
                pltpu.VMEM((V * D, 3 * DE), BF16),
                pltpu.VMEM((DE, 3 * C), BF16),
                pltpu.VMEM((V, R, 3 * RE), BF16),
                pltpu.VMEM((V, RE, 3 * R), BF16),
                pltpu.VMEM((V, 2 * C, 2 * C), BF16),
                pltpu.VMEM((V, 2 * C, 2 * C), BF16),
                pltpu.SMEM((V, 3, TAPS), F32),
                pltpu.SMEM((V,), jnp.int32),
                pltpu.SMEM((2, V), jnp.int32),
                pltpu.SemaphoreType.DMA((SEMS,)),
                pltpu.SemaphoreType.DMA((SEMS,)),
                pltpu.SemaphoreType.DMA((5,)),
            ],
            compiler_params=pltpu.CompilerParams(
                collective_id=0, has_side_effects=True, vmem_limit_bytes=60 * 1024 * 1024
            ),
        )(
            estimate.reshape(D * R, C),
            view_data.reshape(V * D, R, C),
            psf,
            shifts,
            extents.T,
        )
        return flat.reshape(D, R, C)

    placed = (P("zslab", "tile", None), P(None, "zslab", "tile", None), P(), P(), P())
    return jax.shard_map(
        per_device, mesh=mesh, in_specs=placed, out_specs=P("zslab", "tile", None), check_vma=False
    )
```

```python
import functools

import jax
import jax.numpy as jnp
from jax import lax
from jax.experimental import pallas as pl
from jax.experimental.pallas import tpu as pltpu
from jax.sharding import PartitionSpec as P

MESH = pl.DeviceIdType.MESH
V, TAPS, ITERS = 6, 31, 2
H = TAPS // 2
W = 16
D, R, C = 16, 32, 128
DE, RE = D + 2 * W, R + 2 * W
N = 4
ORDER = (0, 28, 4, 24, 8, 20, 12, 16)
SEMS = 2 + 12 * len(ORDER)
F32, BF16 = jnp.float32, jnp.bfloat16


def halves(x):
    hi = x.astype(BF16)
    return hi, (x - hi.astype(F32)).astype(BF16)


def stacked(x):
    hi, lo = halves(x)
    return jnp.concatenate([hi, lo, hi], axis=0)


def dot(a, b):
    return jnp.dot(a, b, preferred_element_type=F32)


def split_part(value):
    hi, lo = halves(value)
    return hi.astype(F32), lo.astype(F32)


def iota(shape, dim):
    return lax.broadcasted_iota(jnp.int32, shape, dim)


def taps(psf, v, a):
    lane = iota((8, C), 1)
    forward = jnp.zeros((8, C), F32)
    reverse = jnp.zeros((8, C), F32)
    for t in range(TAPS):
        p = psf[v, a, t]
        forward = jnp.where(lane == t, p, forward)
        reverse = jnp.where(lane == TAPS - 1 - t, p, reverse)
    weight = jnp.sum(forward, axis=1, keepdims=True)
    return forward / weight, reverse / weight


def slanted(row, rows, first):
    whole = jnp.concatenate([row] * (rows // 8), axis=0)
    return pltpu.roll(whole, first % C, 1, stride=1, stride_axis=0)


def kernel(
    nz, nt, est, view, psf_in, shifts_in, extents_in, out,
    raw, near, ext, zbuf, xbuf, rbuf, back, got_x, got_y, got_n, got_h,
    kz, kzt, kx, kxt, ky, kyt, psf, shifts, extents, send, recv, local,
):
    zs, ti = lax.axis_index("zslab"), lax.axis_index("tile")
    odd = lax.rem(zs, 2)
    mate, ahead, behind = zs + 1 - 2 * odd, zs + 2 - 4 * odd, zs - 2 + 4 * odd
    close = pl.multiple_of(2 * W * (1 - odd), W)
    far = pl.multiple_of(2 * W * odd, W)
    is_mate = mate < nz

    class Sent:
        def __init__(self, number, src, dst, target, exists, comes):
            self.exists, self.comes = exists, comes
            self.copy = pltpu.make_async_remote_copy(
                src_ref=src, dst_ref=dst, send_sem=send.at[number], recv_sem=recv.at[number],
                device_id=target, device_id_type=MESH,
            )

        def start(self):
            pl.when(self.exists)(self.copy.start)

        def sent(self):
            pl.when(self.exists)(self.copy.wait_send)

        def arrived(self, where=True):
            pl.when(self.comes & where)(self.copy.wait_recv)

    is_ahead = (ahead >= 0) & (ahead < nz)
    is_behind = (behind >= 0) & (behind < nz)
    is_left, is_right = ti > 0, ti < nt - 1
    seam = nt // 2 if nz % 2 == 0 else -1
    seam_left, seam_right = is_left & (ti == seam), is_right & (ti == seam - 1)
    left = {"zslab": jnp.where(seam_left, mate, zs), "tile": ti - 1}
    right = {"zslab": jnp.where(seam_right, mate, zs), "tile": ti + 1}
    numbers = iter(range(SEMS))

    def to_mate(src, dst):
        return Sent(next(numbers), src, dst, {"zslab": mate}, is_mate, is_mate)

    def to_ahead(src, dst, where=True):
        return Sent(
            next(numbers), src, dst, {"zslab": ahead}, is_ahead & where, is_behind & where
        )

    def to_behind(src, dst, where=True):
        return Sent(
            next(numbers), src, dst, {"zslab": behind}, is_behind & where, is_ahead & where
        )

    reads = [
        pltpu.make_async_copy(src, dst, local.at[k])
        for k, (src, dst) in enumerate(
            [(est, raw), (view, near.at[:, W : W + R]), (psf_in, psf), (shifts_in, shifts), (extents_in, extents)]
        )
    ]
    for read in reads:
        read.start()

    ext[...] = jnp.zeros(ext.shape, F32)
    got_x[...] = jnp.zeros(got_x.shape, F32)
    got_y[...] = jnp.zeros(got_y.shape, F32)
    got_h[...] = jnp.zeros(got_h.shape, F32)
    near[:, 0:W] = jnp.zeros((V * D, W, C), F32)
    near[:, W + R :] = jnp.zeros((V * D, W, C), F32)
    barrier = pltpu.get_barrier_semaphore()
    beside = [
        ({"zslab": mate}, is_mate), ({"zslab": ahead}, is_ahead), ({"zslab": behind}, is_behind),
        ({"tile": ti - 1}, is_left), ({"tile": ti + 1}, is_right),
        (left, seam_left), (right, seam_right),
    ]
    for target, exists in beside:

        @pl.when(exists)
        def _(target=target):
            pl.semaphore_signal(barrier, inc=1, device_id=target, device_id_type=MESH)

    reads[0].wait()
    for x in range(R):
        ext[W + x, W : W + D] = raw[pl.ds(x, D, stride=R)]
    pl.semaphore_wait(barrier, sum(exists.astype(jnp.int32) for _, exists in beside))

    own_p, close_p, far_p = pl.ds(W, D), pl.ds(close, W), pl.ds(far, W)

    def rows_of(r):
        return slice(W + r, W + r + N)

    def beyond(r):
        return slice(W + R + r, W + R + r + N) if r < W else slice(r - W, r - W + N)

    def crossed(where, p):
        if p is far_p:
            return p
        start, other = (W, far) if p is own_p else (close, W)
        return pl.ds(pl.multiple_of(jnp.where(where, other, start), W), W)

    def to_tile(leftward, src, dst, p):
        seam_out, seam_in = (seam_left, seam_right) if leftward else (seam_right, seam_left)
        exists, comes = (is_left, is_right) if leftward else (is_right, is_left)
        if p is far_p:
            exists, comes = exists & jnp.logical_not(seam_out), comes & jnp.logical_not(seam_in)
        return Sent(
            next(numbers), src, dst.at[:, crossed(seam_out, p)], left if leftward else right, exists, comes
        )

    def est_tile(r, p):
        return to_tile(r < W, ext.at[rows_of(r), p], ext.at[beyond(r)], p)

    def back_tile(r, p):
        return to_tile(r >= W, back.at[beyond(r), p], got_x.at[r : r + N], p)

    def at_seam(r):
        return seam_right if r < W else seam_left

    def by_seam(r):
        return seam_left if r < W else seam_right

    views = [
        Sent(next(numbers), view.at[:, 0:W], near.at[:, W + R : RE], {"tile": ti - 1}, is_left, is_right),
        Sent(next(numbers), view.at[:, R - W : R], near.at[:, 0:W], {"tile": ti + 1}, is_right, is_left),
    ]
    est_mate = {r: to_mate(ext.at[rows_of(r), own_p], ext.at[rows_of(r), far_p]) for r in ORDER}
    est_ahead = {r: to_ahead(ext.at[rows_of(r), close_p], ext.at[rows_of(r), far_p]) for r in ORDER}
    est_halo = {
        r: to_ahead(ext.at[beyond(r), close_p], ext.at[beyond(r), far_p], at_seam(r)) for r in ORDER
    }
    est_own = {r: est_tile(r, own_p) for r in ORDER}
    est_close = {r: est_tile(r, close_p) for r in ORDER}
    est_far = {r: est_tile(r, far_p) for r in ORDER}
    back_halo = {r: to_behind(back.at[beyond(r), far_p], got_h.at[r : r + N], at_seam(r)) for r in ORDER}
    back_far = {r: back_tile(r, far_p) for r in ORDER}
    back_close = {r: back_tile(r, close_p) for r in ORDER}
    back_own = {r: back_tile(r, own_p) for r in ORDER}
    back_behind = {r: to_behind(back.at[rows_of(r), far_p], got_y.at[r : r + N]) for r in ORDER}
    back_mate = {r: to_mate(back.at[rows_of(r), close_p], got_n.at[r : r + N]) for r in ORDER}
    est_sends = [est_mate, est_ahead, est_halo, est_own, est_close, est_far]
    back_sends = [back_halo, back_far, back_close, back_own, back_behind, back_mate]

    def build():
        lane = iota((C, C), 1)
        gap = iota((C, C), 0) - lane
        banded = (gap >= -H) & (gap <= H)

        def one(v, total):
            forward, reverse = taps(psf, v, 2)
            hi, lo = split_part(slanted(forward, D, 1))
            low = pltpu.roll(lo, 2 * DE, 1)
            at = pl.ds(pl.multiple_of(v * D, D), D)
            kz[at, 0:C] = (
                hi + pltpu.roll(hi, DE, 1) + jnp.where(lane[0:D] >= 2 * DE, low, 0.0)
            ).astype(BF16)
            kz[at, C:] = low[:, 0 : 3 * DE - C].astype(BF16)
            z_back = jnp.where(lane[0:DE] < D, slanted(reverse, DE, -TAPS), 0.0)
            forward, reverse = taps(psf, v, 0)
            hi, lo = split_part(slanted(forward, R, 1))
            kx[v, :, 0:C] = (hi + pltpu.roll(hi, RE, 1)).astype(BF16)
            kx[v, :, C:] = lo[:, 0:RE].astype(BF16)
            hi, lo = split_part(jnp.where(lane[0:RE] < R, slanted(reverse, RE, -TAPS), 0.0))
            kxt[v] = (hi + pltpu.roll(hi, R, 1) + pltpu.roll(lo, 2 * R, 1))[:, 0 : 3 * R].astype(BF16)
            forward, reverse = taps(psf, v, 1)
            for mat, row in ((ky, reverse), (kyt, forward)):
                hi, lo = halves(jnp.where(banded, slanted(row, C, -H), 0.0))
                mat[v, 0:C, 0:C] = hi
                mat[v, 0:C, C:] = lo
                mat[v, C:, 0:C] = hi
                mat[v, C:, C:] = jnp.zeros((C, C), BF16)
            return total + pltpu.roll(z_back, v * D, 1)

        hi, lo = split_part(lax.fori_loop(0, V, one, jnp.zeros((DE, C), F32)))
        again, low = pltpu.roll(hi, V * D, 1), pltpu.roll(lo, 2 * V * D - C, 1)
        kzt[:, 0:C] = jnp.where(lane[0:DE] < V * D, hi, again).astype(BF16)
        kzt[:, C : 2 * C] = jnp.where(lane[0:DE] < 2 * V * D - C, again, low).astype(BF16)
        kzt[:, 2 * C :] = low[:, 0 : 3 * V * D - 2 * C].astype(BF16)

    def along_z(i, carry):
        x = 2 * i
        o = dot(kz[...], stacked(jnp.concatenate([ext[x], ext[x + 1]], axis=1)))
        for v in range(V):
            for k in range(2):
                at = pl.multiple_of((x + k) * D, D)
                zbuf[v, pl.ds(at, D)] = o[v * D : (v + 1) * D, k * C : (k + 1) * C]
        return carry

    def one_view(v, carry):
        for i in range(0, D, 2):
            both = [zbuf[v, pl.ds(i + k, RE, stride=D)] for k in range(2)]
            o = dot(kx[v], stacked(jnp.concatenate(both, axis=1)))
            xbuf[i * R : (i + 1) * R] = o[:, :C]
            xbuf[(i + 1) * R : (i + 2) * R] = o[:, C:]
        o = dot(jnp.concatenate(halves(xbuf[...]), axis=1), ky[v])
        blurred = o[:, :C] + o[:, C:]
        start = W + shifts[v]
        for z in range(D):
            plane = zs * D + z
            inside = jnp.where((plane >= extents[0, v]) & (plane < extents[1, v]), 1.0, 0.0)
            data = near[v * D + z, pl.ds(start, R)]
            xbuf[z * R : (z + 1) * R] = inside * data / blurred[z * R : (z + 1) * R]
        o = dot(jnp.concatenate(halves(xbuf[...]), axis=1), kyt[v])
        xbuf[...] = o[:, :C] + o[:, C:]
        for i in range(0, D, 2):
            both = [xbuf[(i + k) * R : (i + k + 1) * R] for k in range(2)]
            o = dot(kxt[v], stacked(jnp.concatenate(both, axis=1)))
            for k in range(2):
                at = pl.multiple_of((v * D + i + k) * RE, RE)
                rbuf[pl.ds(at, RE)] = o[:, k * C : (k + 1) * C]
        return carry

    def along_z_back(i, carry):
        x = 2 * i
        both = [rbuf[pl.ds(x + k, V * D, stride=RE)] for k in range(2)]
        o = dot(kzt[...], stacked(jnp.concatenate(both, axis=1)))
        back[x] = o[:, :C]
        back[x + 1] = o[:, C:]
        return carry

    def over(body, first, rows):
        lax.fori_loop(first // 2, (first + rows) // 2, body, 0, unroll=2)

    for r in ORDER:
        est_mate[r].start()
        est_own[r].start()
    for copy in views:
        copy.start()
    for read in reads[2:]:
        read.wait()
    build()
    depth = zs * D + iota((D, C), 0)
    count = jnp.zeros((D, C), F32)
    for v in range(V):
        held = (depth >= extents[0, v]) & (depth < extents[1, v])
        count = count + jnp.where(held, 1.0, 0.0)

    for step in range(ITERS):
        for r in ORDER:
            est_mate[r].arrived()
            est_ahead[r].start()
            est_close[r].start()
        for r in ORDER:
            est_own[r].arrived(at_seam(r))
            est_halo[r].start()
        for r in ORDER:
            est_ahead[r].arrived()
            est_far[r].start()
            over(along_z, W + r, N)
        for r in ORDER:
            est_own[r].arrived(jnp.logical_not(at_seam(r)))
            est_close[r].arrived()
            est_far[r].arrived()
            est_halo[r].arrived()
            over(along_z, beyond(r).start, N)
        if step == 0:
            reads[1].wait()
            for copy in views:
                copy.arrived()
        lax.fori_loop(0, V, one_view, 0)
        for group in est_sends:
            for r in ORDER:
                group[r].sent()
        for r in ORDER:
            over(along_z_back, beyond(r).start, N)
            back_halo[r].start()
            back_far[r].start()
        for r in ORDER:
            pl.when(jnp.logical_not(at_seam(r)))(back_close[r].start)
        for r in ORDER:
            back_own[r].start()
        over(along_z_back, W, R)
        for r in ORDER:

            @pl.when(at_seam(r))
            def _():
                back_halo[r].arrived()
                back[beyond(r), close_p] += got_h[r : r + N]
                back_close[r].start()

        for r in ORDER:
            back_far[r].arrived()
            back[rows_of(r), far_p] += got_x[r : r + N, far_p]
            back_behind[r].start()
        for r in ORDER:
            back_close[r].arrived(jnp.logical_not(by_seam(r)))
            back_own[r].arrived(by_seam(r))
            back_behind[r].arrived()
            back[rows_of(r), close_p] += got_x[r : r + N, close_p] + got_y[r : r + N]
            back_mate[r].start()
        for r in ORDER:
            back_own[r].arrived(jnp.logical_not(by_seam(r)))
            back_close[r].arrived(by_seam(r))
            back_mate[r].arrived()
            for x in range(r, r + N):
                total = back[W + x, W : W + D] + got_x[x, W : W + D] + got_n[x]
                updated = ext[W + x, W : W + D] * total / count
                if step < ITERS - 1:
                    ext[W + x, W : W + D] = updated
                else:
                    out[pl.ds(x, D, stride=R)] = updated
            if step < ITERS - 1:
                est_mate[r].start()
                est_own[r].start()
        for group in back_sends:
            for r in ORDER:
                group[r].sent()
    for copy in views:
        copy.sent()


def solution(mesh):
    nz, nt = mesh.shape["zslab"], mesh.shape["tile"]

    def per_device(estimate, view_data, psf, shifts, extents):
        flat = pl.pallas_call(
            functools.partial(kernel, nz, nt),
            out_shape=pltpu.VMEM((D * R, C), F32),
            in_specs=[pl.BlockSpec(memory_space=pltpu.HBM)] * 5,
            out_specs=pl.BlockSpec(memory_space=pltpu.VMEM),
            scratch_shapes=[
                pltpu.VMEM((D * R, C), F32),
                pltpu.VMEM((V * D, RE, C), F32),
                pltpu.VMEM((RE, DE, C), F32),
                pltpu.VMEM((V, RE * D, C), F32),
                pltpu.VMEM((D * R, C), F32),
                pltpu.VMEM((V * D * RE, C), F32),
                pltpu.VMEM((RE, DE, C), F32),
                pltpu.VMEM((R, DE, C), F32),
                pltpu.VMEM((R, D, C), F32),
                pltpu.VMEM((R, D, C), F32),
                pltpu.VMEM((R, D, C), F32),
                pltpu.VMEM((V * D, 3 * DE), BF16),
                pltpu.VMEM((DE, 3 * V * D), BF16),
                pltpu.VMEM((V, R, 3 * RE), BF16),
                pltpu.VMEM((V, RE, 3 * R), BF16),
                pltpu.VMEM((V, 2 * C, 2 * C), BF16),
                pltpu.VMEM((V, 2 * C, 2 * C), BF16),
                pltpu.SMEM((V, 3, TAPS), F32),
                pltpu.SMEM((V,), jnp.int32),
                pltpu.SMEM((2, V), jnp.int32),
                pltpu.SemaphoreType.DMA((SEMS,)),
                pltpu.SemaphoreType.DMA((SEMS,)),
                pltpu.SemaphoreType.DMA((5,)),
            ],
            compiler_params=pltpu.CompilerParams(
                collective_id=0, has_side_effects=True, vmem_limit_bytes=60 * 1024 * 1024
            ),
        )(
            estimate.reshape(D * R, C),
            view_data.reshape(V * D, R, C),
            psf,
            shifts,
            extents.T,
        )
        return flat.reshape(D, R, C)

    placed = (P("zslab", "tile", None), P(None, "zslab", "tile", None), P(), P(), P())
    return jax.shard_map(
        per_device, mesh=mesh, in_specs=placed, out_specs=P("zslab", "tile", None), check_vma=False
    )
```

```python
import functools

import jax
import jax.numpy as jnp
from jax import lax
from jax.experimental import pallas as pl
from jax.experimental.pallas import tpu as pltpu
from jax.sharding import PartitionSpec as P

MESH = pl.DeviceIdType.MESH
V, TAPS, ITERS = 6, 31, 2
H = TAPS // 2
W = 16
D, R, C = 16, 32, 128
DE, RE = D + 2 * W, R + 2 * W
N = 4
ORDER = (0, 28, 4, 24, 8, 20, 12, 16)
GROUPS = ((0, 4), (24, 28), (8, 12), (16, 20))
SIDES = ((0, 4, 8, 12), (16, 20, 24, 28))
DIRECT = 2
SEMS = 2 + 12 * len(ORDER)
F32, BF16 = jnp.float32, jnp.bfloat16


def halves(x):
    hi = x.astype(BF16)
    return hi, (x - hi.astype(F32)).astype(BF16)


def stacked(x):
    hi, lo = halves(x)
    return jnp.concatenate([hi, lo, hi], axis=0)


def dot(a, b):
    return jnp.dot(a, b, preferred_element_type=F32)


def split_part(value):
    hi, lo = halves(value)
    return hi.astype(F32), lo.astype(F32)


def iota(shape, dim):
    return lax.broadcasted_iota(jnp.int32, shape, dim)


def taps(psf, v, a):
    lane = iota((8, C), 1)
    forward = jnp.zeros((8, C), F32)
    reverse = jnp.zeros((8, C), F32)
    for t in range(TAPS):
        p = psf[v, a, t]
        forward = jnp.where(lane == t, p, forward)
        reverse = jnp.where(lane == TAPS - 1 - t, p, reverse)
    weight = jnp.sum(forward, axis=1, keepdims=True)
    return forward / weight, reverse / weight


def slanted(row, rows, first):
    whole = jnp.concatenate([row] * (rows // 8), axis=0)
    return pltpu.roll(whole, first % C, 1, stride=1, stride_axis=0)


def kernel(
    nz, nt, est, view, psf_in, shifts_in, extents_in, out,
    raw, near, ext, zbuf, xbuf, rbuf, back, got_x, got_y, got_n, got_h,
    kz, kzt, kx, kxt, ky, kyt, psf, shifts, extents, send, recv, local,
):
    zs, ti = lax.axis_index("zslab"), lax.axis_index("tile")
    odd = lax.rem(zs, 2)
    mate, ahead, behind = zs + 1 - 2 * odd, zs + 2 - 4 * odd, zs - 2 + 4 * odd
    other = zs - 1 + 2 * odd
    close = pl.multiple_of(2 * W * (1 - odd), W)
    far = pl.multiple_of(2 * W * odd, W)
    is_mate = mate < nz

    class Sent:
        def __init__(self, number, src, dst, target, exists, comes):
            self.exists, self.comes = exists, comes
            self.copy = pltpu.make_async_remote_copy(
                src_ref=src, dst_ref=dst, send_sem=send.at[number], recv_sem=recv.at[number],
                device_id=target, device_id_type=MESH,
            )

        def start(self):
            pl.when(self.exists)(self.copy.start)

        def sent(self):
            pl.when(self.exists)(self.copy.wait_send)

        def arrived(self, where=True):
            pl.when(self.comes & where)(self.copy.wait_recv)

    is_ahead = (ahead >= 0) & (ahead < nz)
    is_behind = (behind >= 0) & (behind < nz)
    is_other = (other >= 0) & (other < nz)
    is_left, is_right = ti > 0, ti < nt - 1
    seam = nt // 2 if nz % 2 == 0 else -1
    seam_left, seam_right = is_left & (ti == seam), is_right & (ti == seam - 1)
    left = {"zslab": jnp.where(seam_left, mate, zs), "tile": ti - 1}
    right = {"zslab": jnp.where(seam_right, mate, zs), "tile": ti + 1}
    numbers = iter(range(SEMS))

    def to_mate(src, dst):
        return Sent(next(numbers), src, dst, {"zslab": mate}, is_mate, is_mate)

    def to_other(src, dst):
        return Sent(next(numbers), src, dst, {"zslab": other}, is_other, is_other)

    def to_ahead(src, dst, where=True):
        return Sent(
            next(numbers), src, dst, {"zslab": ahead}, is_ahead & where, is_behind & where
        )

    def to_behind(src, dst, where=True):
        return Sent(
            next(numbers), src, dst, {"zslab": behind}, is_behind & where, is_ahead & where
        )

    reads = [
        pltpu.make_async_copy(src, dst, local.at[k])
        for k, (src, dst) in enumerate(
            [(est, raw), (view, near.at[:, W : W + R]), (psf_in, psf), (shifts_in, shifts), (extents_in, extents)]
        )
    ]
    for read in reads:
        read.start()

    ext[...] = jnp.zeros(ext.shape, F32)
    got_x[...] = jnp.zeros(got_x.shape, F32)
    got_y[...] = jnp.zeros(got_y.shape, F32)
    got_h[...] = jnp.zeros(got_h.shape, F32)
    near[:, 0:W] = jnp.zeros((V * D, W, C), F32)
    near[:, W + R :] = jnp.zeros((V * D, W, C), F32)
    barrier = pltpu.get_barrier_semaphore()
    beside = [
        ({"zslab": mate}, is_mate), ({"zslab": other}, is_other), ({"zslab": ahead}, is_ahead), ({"zslab": behind}, is_behind),
        ({"tile": ti - 1}, is_left), ({"tile": ti + 1}, is_right),
        (left, seam_left), (right, seam_right),
    ]
    for target, exists in beside:

        @pl.when(exists)
        def _(target=target):
            pl.semaphore_signal(barrier, inc=1, device_id=target, device_id_type=MESH)

    reads[0].wait()
    for x in range(R):
        ext[W + x, W : W + D] = raw[pl.ds(x, D, stride=R)]
    pl.semaphore_wait(barrier, sum(exists.astype(jnp.int32) for _, exists in beside))

    own_p, close_p, far_p = pl.ds(W, D), pl.ds(close, W), pl.ds(far, W)

    def rows_of(r):
        return slice(W + r, W + r + N)

    def beyond(r):
        return slice(W + R + r, W + R + r + N) if r < W else slice(r - W, r - W + N)

    def crossed(where, p):
        if p is far_p:
            return p
        start, other = (W, far) if p is own_p else (close, W)
        return pl.ds(pl.multiple_of(jnp.where(where, other, start), W), W)

    def to_tile(leftward, src, dst, p):
        seam_out, seam_in = (seam_left, seam_right) if leftward else (seam_right, seam_left)
        exists, comes = (is_left, is_right) if leftward else (is_right, is_left)
        if p is far_p:
            exists, comes = exists & jnp.logical_not(seam_out), comes & jnp.logical_not(seam_in)
        return Sent(
            next(numbers), src, dst.at[:, crossed(seam_out, p)], left if leftward else right, exists, comes
        )

    def est_tile(r, p):
        return to_tile(r < W, ext.at[rows_of(r), p], ext.at[beyond(r)], p)

    def back_tile(r, p):
        return to_tile(r >= W, back.at[beyond(r), p], got_x.at[r : r + N], p)

    def at_seam(r):
        return seam_right if r < W else seam_left

    def by_seam(r):
        return seam_left if r < W else seam_right

    views = [
        Sent(next(numbers), view.at[:, 0:W], near.at[:, W + R : RE], {"tile": ti - 1}, is_left, is_right),
        Sent(next(numbers), view.at[:, R - W : R], near.at[:, 0:W], {"tile": ti + 1}, is_right, is_left),
    ]
    est_mate = {r: to_mate(ext.at[rows_of(r), own_p], ext.at[rows_of(r), far_p]) for r in ORDER}
    est_ahead = {
        r: to_ahead(ext.at[rows_of(r), close_p], ext.at[rows_of(r), far_p]) for r in ORDER[:-DIRECT]
    }
    est_direct = {
        r: to_other(ext.at[rows_of(r), own_p], ext.at[rows_of(r), close_p]) for r in ORDER[-DIRECT:]
    }
    est_third = est_ahead | est_direct
    est_halo = {
        r: to_ahead(ext.at[beyond(r), close_p], ext.at[beyond(r), far_p], at_seam(r)) for r in ORDER
    }
    est_own = {r: est_tile(r, own_p) for r in ORDER}
    est_close = {r: est_tile(r, close_p) for r in ORDER}
    est_far = {r: est_tile(r, far_p) for r in ORDER}
    back_halo = {r: to_behind(back.at[beyond(r), far_p], got_h.at[r : r + N], at_seam(r)) for r in ORDER}
    back_far = {r: back_tile(r, far_p) for r in ORDER}
    back_close = {r: back_tile(r, close_p) for r in ORDER}
    back_own = {r: back_tile(r, own_p) for r in ORDER}
    back_behind = {
        r: to_behind(back.at[rows_of(r), far_p], got_y.at[r : r + N]) for r in ORDER[DIRECT:]
    }
    back_direct = {
        r: to_other(back.at[rows_of(r), far_p], got_y.at[r : r + N]) for r in ORDER[:DIRECT]
    }
    back_third = back_behind | back_direct
    back_mate = {r: to_mate(back.at[rows_of(r), close_p], got_n.at[r : r + N]) for r in ORDER}
    est_sends = [est_mate, est_third, est_halo, est_own, est_close, est_far]
    back_sends = [back_halo, back_far, back_close, back_own, back_third, back_mate]

    def build():
        lane = iota((C, C), 1)
        gap = iota((C, C), 0) - lane
        banded = (gap >= -H) & (gap <= H)

        def one(v, total):
            forward, reverse = taps(psf, v, 2)
            hi, lo = split_part(slanted(forward, D, 1))
            low = pltpu.roll(lo, 2 * DE, 1)
            at = pl.ds(pl.multiple_of(v * D, D), D)
            kz[at, 0:C] = (
                hi + pltpu.roll(hi, DE, 1) + jnp.where(lane[0:D] >= 2 * DE, low, 0.0)
            ).astype(BF16)
            kz[at, C:] = low[:, 0 : 3 * DE - C].astype(BF16)
            z_back = jnp.where(lane[0:DE] < D, slanted(reverse, DE, -TAPS), 0.0)
            forward, reverse = taps(psf, v, 0)
            hi, lo = split_part(slanted(forward, R, 1))
            kx[v, :, 0:C] = (hi + pltpu.roll(hi, RE, 1)).astype(BF16)
            kx[v, :, C:] = lo[:, 0:RE].astype(BF16)
            hi, lo = split_part(jnp.where(lane[0:RE] < R, slanted(reverse, RE, -TAPS), 0.0))
            kxt[v] = (hi + pltpu.roll(hi, R, 1) + pltpu.roll(lo, 2 * R, 1))[:, 0 : 3 * R].astype(BF16)
            forward, reverse = taps(psf, v, 1)
            for mat, row in ((ky, reverse), (kyt, forward)):
                hi, lo = halves(jnp.where(banded, slanted(row, C, -H), 0.0))
                mat[v, 0:C, 0:C] = hi
                mat[v, 0:C, C:] = lo
                mat[v, C:, 0:C] = hi
                mat[v, C:, C:] = jnp.zeros((C, C), BF16)
            return total + pltpu.roll(z_back, v * D, 1)

        hi, lo = split_part(lax.fori_loop(0, V, one, jnp.zeros((DE, C), F32)))
        again, low = pltpu.roll(hi, V * D, 1), pltpu.roll(lo, 2 * V * D - C, 1)
        kzt[:, 0:C] = jnp.where(lane[0:DE] < V * D, hi, again).astype(BF16)
        kzt[:, C : 2 * C] = jnp.where(lane[0:DE] < 2 * V * D - C, again, low).astype(BF16)
        kzt[:, 2 * C :] = low[:, 0 : 3 * V * D - 2 * C].astype(BF16)

    def along_z(i, carry):
        x = 2 * i
        o = dot(kz[...], stacked(jnp.concatenate([ext[x], ext[x + 1]], axis=1)))
        for v in range(V):
            for k in range(2):
                at = (x + k) * D
                zbuf[v, pl.ds(at, D)] = o[v * D : (v + 1) * D, k * C : (k + 1) * C]
        return carry

    def one_view(v, carry):
        for i in range(0, D, 2):
            both = [zbuf[v, pl.ds(i + k, RE, stride=D)] for k in range(2)]
            o = dot(kx[v], stacked(jnp.concatenate(both, axis=1)))
            xbuf[v, i * R : (i + 1) * R] = o[:, :C]
            xbuf[v, (i + 1) * R : (i + 2) * R] = o[:, C:]
        o = dot(jnp.concatenate(halves(xbuf[v]), axis=1), ky[v])
        blurred = o[:, :C] + o[:, C:]
        start = W + shifts[v]
        for z in range(D):
            plane = zs * D + z
            inside = jnp.where((plane >= extents[0, v]) & (plane < extents[1, v]), 1.0, 0.0)
            data = near[v * D + z, pl.ds(start, R)]
            xbuf[v, z * R : (z + 1) * R] = inside * data / blurred[z * R : (z + 1) * R]
        o = dot(jnp.concatenate(halves(xbuf[v]), axis=1), kyt[v])
        xbuf[v] = o[:, :C] + o[:, C:]
        for i in range(0, D, 2):
            both = [xbuf[v, (i + k) * R : (i + k + 1) * R] for k in range(2)]
            o = dot(kxt[v], stacked(jnp.concatenate(both, axis=1)))
            for k in range(2):
                at = pl.multiple_of((v * D + i + k) * RE, RE)
                rbuf[pl.ds(at, RE)] = o[:, k * C : (k + 1) * C]
        return carry

    def along_z_back(i, carry):
        x = 2 * i
        both = [rbuf[pl.ds(x + k, V * D, stride=RE)] for k in range(2)]
        o = dot(kzt[...], stacked(jnp.concatenate(both, axis=1)))
        back[x] = o[:, :C]
        back[x + 1] = o[:, C:]
        return carry

    def over(body, first, rows):
        for i in range(first // 2, (first + rows) // 2):
            body(i, 0)

    for r in ORDER:
        est_mate[r].start()
        est_own[r].start()
    for copy in est_direct.values():
        copy.start()
    for copy in views:
        copy.start()
    for read in reads[2:]:
        read.wait()
    build()
    depth = zs * D + iota((D, C), 0)
    count = jnp.zeros((D, C), F32)
    for v in range(V):
        held = (depth >= extents[0, v]) & (depth < extents[1, v])
        count = count + jnp.where(held, 1.0, 0.0)

    for step in range(ITERS):
        for r in ORDER:
            est_mate[r].arrived()
            if r in est_ahead:
                est_ahead[r].start()
            est_close[r].start()
        for r in ORDER:
            est_own[r].arrived(at_seam(r))
            est_halo[r].start()
        for r in ORDER:
            est_third[r].arrived()
            est_far[r].start()
        over(along_z, W, R)
        for side in SIDES:
            for r in side:
                est_own[r].arrived(jnp.logical_not(at_seam(r)))
                est_close[r].arrived()
                est_far[r].arrived()
                est_halo[r].arrived()
            over(along_z, beyond(min(side)).start, N * len(side))
        if step == 0:
            reads[1].wait()
            for copy in views:
                copy.arrived()
        lax.fori_loop(0, V, one_view, 0, unroll=2)
        for group in est_sends:
            for r in ORDER:
                group[r].sent()
        for group in GROUPS:
            over(along_z_back, beyond(min(group)).start, N * len(group))
            for r in group:
                back_halo[r].start()
                back_far[r].start()
        for r in ORDER:
            pl.when(jnp.logical_not(at_seam(r)))(back_close[r].start)
        for r in ORDER:
            back_own[r].start()
        over(along_z_back, W, R)
        for r in ORDER:

            @pl.when(at_seam(r))
            def _():
                back_halo[r].arrived()
                back[beyond(r), close_p] += got_h[r : r + N]
                back_close[r].start()

        for r in ORDER:
            back_far[r].arrived()
            back[rows_of(r), far_p] += got_x[r : r + N, far_p]
            back_third[r].start()
        for r in ORDER:
            back_close[r].arrived(jnp.logical_not(by_seam(r)))
            back_own[r].arrived(by_seam(r))
            if r in back_behind:
                back_behind[r].arrived()
                back[rows_of(r), close_p] += got_x[r : r + N, close_p] + got_y[r : r + N]
            else:
                back[rows_of(r), close_p] += got_x[r : r + N, close_p]
            back_mate[r].start()
        for r in ORDER:
            back_own[r].arrived(jnp.logical_not(by_seam(r)))
            back_close[r].arrived(by_seam(r))
            back_mate[r].arrived()
            if r in back_direct:
                back_direct[r].arrived()
            for x in range(r, r + N):
                total = back[W + x, W : W + D] + got_x[x, W : W + D] + got_n[x]
                if r in back_direct:
                    total = total + got_y[x]
                updated = ext[W + x, W : W + D] * total / count
                if step < ITERS - 1:
                    ext[W + x, W : W + D] = updated
                else:
                    out[pl.ds(x, D, stride=R)] = updated
            if step < ITERS - 1:
                est_mate[r].start()
                est_own[r].start()
                if r in est_direct:
                    est_direct[r].start()
        for group in back_sends:
            for r in ORDER:
                group[r].sent()
    for copy in views:
        copy.sent()


def solution(mesh):
    nz, nt = mesh.shape["zslab"], mesh.shape["tile"]

    def per_device(estimate, view_data, psf, shifts, extents):
        flat = pl.pallas_call(
            functools.partial(kernel, nz, nt),
            out_shape=pltpu.VMEM((D * R, C), F32),
            in_specs=[pl.BlockSpec(memory_space=pltpu.HBM)] * 5,
            out_specs=pl.BlockSpec(memory_space=pltpu.VMEM),
            scratch_shapes=[
                pltpu.VMEM((D * R, C), F32),
                pltpu.VMEM((V * D, RE, C), F32),
                pltpu.VMEM((RE, DE, C), F32),
                pltpu.VMEM((V, RE * D, C), F32),
                pltpu.VMEM((V, D * R, C), F32),
                pltpu.VMEM((V * D * RE, C), F32),
                pltpu.VMEM((RE, DE, C), F32),
                pltpu.VMEM((R, DE, C), F32),
                pltpu.VMEM((R, D, C), F32),
                pltpu.VMEM((R, D, C), F32),
                pltpu.VMEM((R, D, C), F32),
                pltpu.VMEM((V * D, 3 * DE), BF16),
                pltpu.VMEM((DE, 3 * V * D), BF16),
                pltpu.VMEM((V, R, 3 * RE), BF16),
                pltpu.VMEM((V, RE, 3 * R), BF16),
                pltpu.VMEM((V, 2 * C, 2 * C), BF16),
                pltpu.VMEM((V, 2 * C, 2 * C), BF16),
                pltpu.SMEM((V, 3, TAPS), F32),
                pltpu.SMEM((V,), jnp.int32),
                pltpu.SMEM((2, V), jnp.int32),
                pltpu.SemaphoreType.DMA((SEMS,)),
                pltpu.SemaphoreType.DMA((SEMS,)),
                pltpu.SemaphoreType.DMA((5,)),
            ],
            compiler_params=pltpu.CompilerParams(
                collective_id=0, has_side_effects=True, vmem_limit_bytes=60 * 1024 * 1024
            ),
        )(
            estimate.reshape(D * R, C),
            view_data.reshape(V * D, R, C),
            psf,
            shifts,
            extents.T,
        )
        return flat.reshape(D, R, C)

    placed = (P("zslab", "tile", None), P(None, "zslab", "tile", None), P(), P(), P())
    return jax.shard_map(
        per_device, mesh=mesh, in_specs=placed, out_specs=P("zslab", "tile", None), check_vma=False
    )
```

```python
import functools

import jax
import jax.numpy as jnp
from jax import lax
from jax.experimental import pallas as pl
from jax.experimental.pallas import tpu as pltpu
from jax.sharding import PartitionSpec as P

MESH = pl.DeviceIdType.MESH
V, TAPS, ITERS = 6, 31, 2
H = TAPS // 2
W = 16
D, R, C = 16, 32, 128
DE, RE = D + 2 * W, R + 2 * W
N = 4
ORDER = (0, 28, 4, 24, 8, 20, 12, 16)
GROUPS = ((0, 4), (24, 28), (8, 12), (16, 20))
SIDES = ((0, 4, 8, 12), (16, 20, 24, 28))
DIRECT = 2
SEMS = 2 + 12 * len(ORDER)
F32, BF16 = jnp.float32, jnp.bfloat16


def halves(x):
    hi = x.astype(BF16)
    return hi, (x - hi.astype(F32)).astype(BF16)


def stacked(x):
    hi, lo = halves(x)
    return jnp.concatenate([hi, lo, hi], axis=0)


def dot(a, b):
    return jnp.dot(a, b, preferred_element_type=F32)


def split_part(value):
    hi, lo = halves(value)
    return hi.astype(F32), lo.astype(F32)


def iota(shape, dim):
    return lax.broadcasted_iota(jnp.int32, shape, dim)


def taps(psf, v, a):
    lane = iota((8, C), 1)
    forward = jnp.zeros((8, C), F32)
    reverse = jnp.zeros((8, C), F32)
    for t in range(TAPS):
        p = psf[v, a, t]
        forward = jnp.where(lane == t, p, forward)
        reverse = jnp.where(lane == TAPS - 1 - t, p, reverse)
    weight = jnp.sum(forward, axis=1, keepdims=True)
    return forward / weight, reverse / weight


def slanted(row, rows, first):
    whole = jnp.concatenate([row] * (rows // 8), axis=0)
    return pltpu.roll(whole, first % C, 1, stride=1, stride_axis=0)


def kernel(
    nz, nt, est, view, psf_in, shifts_in, extents_in, out,
    raw, near, ext, zbuf, xbuf, rbuf, back, got_x, got_y, got_n, got_h,
    kz, kzt, kx, kxt, ky, kyt, psf, shifts, extents, send, recv, local,
):
    zs, ti = lax.axis_index("zslab"), lax.axis_index("tile")
    odd = lax.rem(zs, 2)
    mate, ahead, behind = zs + 1 - 2 * odd, zs + 2 - 4 * odd, zs - 2 + 4 * odd
    other = zs - 1 + 2 * odd
    close = pl.multiple_of(2 * W * (1 - odd), W)
    far = pl.multiple_of(2 * W * odd, W)
    is_mate = mate < nz

    class Sent:
        def __init__(self, number, src, dst, target, exists, comes):
            self.exists, self.comes = exists, comes
            self.copy = pltpu.make_async_remote_copy(
                src_ref=src, dst_ref=dst, send_sem=send.at[number], recv_sem=recv.at[number],
                device_id=target, device_id_type=MESH,
            )

        def start(self):
            pl.when(self.exists)(self.copy.start)

        def sent(self):
            pl.when(self.exists)(self.copy.wait_send)

        def arrived(self, where=True):
            pl.when(self.comes & where)(self.copy.wait_recv)

    is_ahead = (ahead >= 0) & (ahead < nz)
    is_behind = (behind >= 0) & (behind < nz)
    is_other = (other >= 0) & (other < nz)
    is_left, is_right = ti > 0, ti < nt - 1
    seam = nt // 2 if nz % 2 == 0 else -1
    seam_left, seam_right = is_left & (ti == seam), is_right & (ti == seam - 1)
    left = {"zslab": jnp.where(seam_left, mate, zs), "tile": ti - 1}
    right = {"zslab": jnp.where(seam_right, mate, zs), "tile": ti + 1}
    numbers = iter(range(SEMS))

    def to_mate(src, dst):
        return Sent(next(numbers), src, dst, {"zslab": mate}, is_mate, is_mate)

    def to_other(src, dst):
        return Sent(next(numbers), src, dst, {"zslab": other}, is_other, is_other)

    def to_ahead(src, dst, where=True):
        return Sent(
            next(numbers), src, dst, {"zslab": ahead}, is_ahead & where, is_behind & where
        )

    def to_behind(src, dst, where=True):
        return Sent(
            next(numbers), src, dst, {"zslab": behind}, is_behind & where, is_ahead & where
        )

    reads = [
        pltpu.make_async_copy(src, dst, local.at[k])
        for k, (src, dst) in enumerate(
            [(est, raw), (view, near.at[:, W : W + R]), (psf_in, psf), (shifts_in, shifts), (extents_in, extents)]
        )
    ]
    for read in reads:
        read.start()

    ext[...] = jnp.zeros(ext.shape, F32)
    got_x[...] = jnp.zeros(got_x.shape, F32)
    got_y[...] = jnp.zeros(got_y.shape, F32)
    got_h[...] = jnp.zeros(got_h.shape, F32)
    near[:, 0:W] = jnp.zeros((V * D, W, C), F32)
    near[:, W + R :] = jnp.zeros((V * D, W, C), F32)
    barrier = pltpu.get_barrier_semaphore()
    beside = [
        ({"zslab": mate}, is_mate), ({"zslab": other}, is_other), ({"zslab": ahead}, is_ahead), ({"zslab": behind}, is_behind),
        ({"tile": ti - 1}, is_left), ({"tile": ti + 1}, is_right),
        (left, seam_left), (right, seam_right),
    ]
    for target, exists in beside:

        @pl.when(exists)
        def _(target=target):
            pl.semaphore_signal(barrier, inc=1, device_id=target, device_id_type=MESH)

    reads[0].wait()
    for x in range(R):
        ext[W + x, W : W + D] = raw[pl.ds(x, D, stride=R)]
    pl.semaphore_wait(barrier, sum(exists.astype(jnp.int32) for _, exists in beside))

    own_p, close_p, far_p = pl.ds(W, D), pl.ds(close, W), pl.ds(far, W)

    def rows_of(r):
        return slice(W + r, W + r + N)

    def beyond(r):
        return slice(W + R + r, W + R + r + N) if r < W else slice(r - W, r - W + N)

    def crossed(where, p):
        if p is far_p:
            return p
        start, other = (W, far) if p is own_p else (close, W)
        return pl.ds(pl.multiple_of(jnp.where(where, other, start), W), W)

    def to_tile(leftward, src, dst, p):
        seam_out, seam_in = (seam_left, seam_right) if leftward else (seam_right, seam_left)
        exists, comes = (is_left, is_right) if leftward else (is_right, is_left)
        if p is far_p:
            exists, comes = exists & jnp.logical_not(seam_out), comes & jnp.logical_not(seam_in)
        return Sent(
            next(numbers), src, dst.at[:, crossed(seam_out, p)], left if leftward else right, exists, comes
        )

    def est_tile(r, p):
        return to_tile(r < W, ext.at[rows_of(r), p], ext.at[beyond(r)], p)

    def back_tile(r, p):
        return to_tile(r >= W, back.at[beyond(r), p], got_x.at[r : r + N], p)

    def at_seam(r):
        return seam_right if r < W else seam_left

    def by_seam(r):
        return seam_left if r < W else seam_right

    views = [
        Sent(next(numbers), view.at[:, 0:W], near.at[:, W + R : RE], {"tile": ti - 1}, is_left, is_right),
        Sent(next(numbers), view.at[:, R - W : R], near.at[:, 0:W], {"tile": ti + 1}, is_right, is_left),
    ]
    est_mate = {r: to_mate(ext.at[rows_of(r), own_p], ext.at[rows_of(r), far_p]) for r in ORDER}
    est_ahead = {
        r: to_ahead(ext.at[rows_of(r), close_p], ext.at[rows_of(r), far_p]) for r in ORDER[:-DIRECT]
    }
    est_direct = {
        r: to_other(ext.at[rows_of(r), own_p], ext.at[rows_of(r), close_p]) for r in ORDER[-DIRECT:]
    }
    est_third = est_ahead | est_direct
    est_halo = {
        r: to_ahead(ext.at[beyond(r), close_p], ext.at[beyond(r), far_p], at_seam(r)) for r in ORDER
    }
    est_own = {r: est_tile(r, own_p) for r in ORDER}
    est_close = {r: est_tile(r, close_p) for r in ORDER}
    est_far = {r: est_tile(r, far_p) for r in ORDER}
    back_halo = {r: to_behind(back.at[beyond(r), far_p], got_h.at[r : r + N], at_seam(r)) for r in ORDER}
    back_far = {r: back_tile(r, far_p) for r in ORDER}
    back_close = {r: back_tile(r, close_p) for r in ORDER}
    back_own = {r: back_tile(r, own_p) for r in ORDER}
    back_behind = {
        r: to_behind(back.at[rows_of(r), far_p], got_y.at[r : r + N]) for r in ORDER[DIRECT:]
    }
    back_direct = {
        r: to_other(back.at[rows_of(r), far_p], got_y.at[r : r + N]) for r in ORDER[:DIRECT]
    }
    back_third = back_behind | back_direct
    back_mate = {r: to_mate(back.at[rows_of(r), close_p], got_n.at[r : r + N]) for r in ORDER}
    est_sends = [est_mate, est_third, est_halo, est_own, est_close, est_far]
    back_sends = [back_halo, back_far, back_close, back_own, back_third, back_mate]

    def build():
        lane = iota((C, C), 1)
        gap = iota((C, C), 0) - lane
        banded = (gap >= -H) & (gap <= H)

        def one(v, total):
            forward, reverse = taps(psf, v, 2)
            hi, lo = split_part(slanted(forward, D, 1))
            low = pltpu.roll(lo, 2 * DE, 1)
            at = pl.ds(pl.multiple_of(v * D, D), D)
            kz[at, 0:C] = (
                hi + pltpu.roll(hi, DE, 1) + jnp.where(lane[0:D] >= 2 * DE, low, 0.0)
            ).astype(BF16)
            kz[at, C:] = low[:, 0 : 3 * DE - C].astype(BF16)
            z_back = jnp.where(lane[0:DE] < D, slanted(reverse, DE, -TAPS), 0.0)
            forward, reverse = taps(psf, v, 0)
            hi, lo = split_part(slanted(forward, R, 1))
            kx[v, :, 0:C] = (hi + pltpu.roll(hi, RE, 1)).astype(BF16)
            kx[v, :, C:] = lo[:, 0:RE].astype(BF16)
            hi, lo = split_part(jnp.where(lane[0:RE] < R, slanted(reverse, RE, -TAPS), 0.0))
            kxt[v] = (hi + pltpu.roll(hi, R, 1) + pltpu.roll(lo, 2 * R, 1))[:, 0 : 3 * R].astype(BF16)
            forward, reverse = taps(psf, v, 1)
            for mat, row in ((ky, reverse), (kyt, forward)):
                hi, lo = halves(jnp.where(banded, slanted(row, C, -H), 0.0))
                mat[v, 0:C, 0:C] = hi
                mat[v, 0:C, C:] = lo
                mat[v, C:, 0:C] = hi
                mat[v, C:, C:] = jnp.zeros((C, C), BF16)
            return total + pltpu.roll(z_back, v * D, 1)

        hi, lo = split_part(lax.fori_loop(0, V, one, jnp.zeros((DE, C), F32)))
        again, low = pltpu.roll(hi, V * D, 1), pltpu.roll(lo, 2 * V * D - C, 1)
        kzt[:, 0:C] = jnp.where(lane[0:DE] < V * D, hi, again).astype(BF16)
        kzt[:, C : 2 * C] = jnp.where(lane[0:DE] < 2 * V * D - C, again, low).astype(BF16)
        kzt[:, 2 * C :] = low[:, 0 : 3 * V * D - 2 * C].astype(BF16)

    def along_z(i, carry):
        x = 2 * i
        o = dot(kz[...], stacked(jnp.concatenate([ext[x], ext[x + 1]], axis=1)))
        for v in range(V):
            for k in range(2):
                at = (x + k) * D
                zbuf[v, pl.ds(at, D)] = o[v * D : (v + 1) * D, k * C : (k + 1) * C]
        return carry

    def one_view(v, carry):
        for i in range(0, D, 2):
            both = [zbuf[v, pl.ds(i + k, RE, stride=D)] for k in range(2)]
            o = dot(kx[v], stacked(jnp.concatenate(both, axis=1)))
            xbuf[v, i * R : (i + 1) * R] = o[:, :C]
            xbuf[v, (i + 1) * R : (i + 2) * R] = o[:, C:]
        o = dot(jnp.concatenate(halves(xbuf[v]), axis=1), ky[v])
        blurred = o[:, :C] + o[:, C:]
        start = W + shifts[v]
        for z in range(D):
            plane = zs * D + z
            inside = jnp.where((plane >= extents[0, v]) & (plane < extents[1, v]), 1.0, 0.0)
            data = near[v * D + z, pl.ds(start, R)]
            xbuf[v, z * R : (z + 1) * R] = inside * data / blurred[z * R : (z + 1) * R]
        o = dot(jnp.concatenate(halves(xbuf[v]), axis=1), kyt[v])
        xbuf[v] = o[:, :C] + o[:, C:]
        for i in range(0, D, 2):
            both = [xbuf[v, (i + k) * R : (i + k + 1) * R] for k in range(2)]
            o = dot(kxt[v], stacked(jnp.concatenate(both, axis=1)))
            for k in range(2):
                at = pl.multiple_of((v * D + i + k) * RE, RE)
                rbuf[pl.ds(at, RE)] = o[:, k * C : (k + 1) * C]
        return carry

    def along_z_back(i, carry):
        x = 2 * i
        both = [rbuf[pl.ds(x + k, V * D, stride=RE)] for k in range(2)]
        o = dot(kzt[...], stacked(jnp.concatenate(both, axis=1)))
        back[x] = o[:, :C]
        back[x + 1] = o[:, C:]
        return carry

    def over(body, first, rows):
        for i in range(first // 2, (first + rows) // 2):
            body(i, 0)

    for r in ORDER:
        est_mate[r].start()
        est_own[r].start()
    for copy in est_direct.values():
        copy.start()
    for copy in views:
        copy.start()
    for read in reads[2:]:
        read.wait()
    build()
    depth = zs * D + iota((D, C), 0)
    count = jnp.zeros((D, C), F32)
    for v in range(V):
        held = (depth >= extents[0, v]) & (depth < extents[1, v])
        count = count + jnp.where(held, 1.0, 0.0)

    for step in range(ITERS):
        for r in ORDER:
            est_mate[r].arrived()
            if r in est_ahead:
                est_ahead[r].start()
            est_close[r].start()
        for r in ORDER:
            est_own[r].arrived(at_seam(r))
            est_halo[r].start()
        for r in ORDER:
            est_third[r].arrived()
            est_far[r].start()
        over(along_z, W, R)
        for side in SIDES:
            for r in side:
                est_own[r].arrived(jnp.logical_not(at_seam(r)))
                est_close[r].arrived()
                est_far[r].arrived()
                est_halo[r].arrived()
            over(along_z, beyond(min(side)).start, N * len(side))
        if step == 0:
            reads[1].wait()
            for copy in views:
                copy.arrived()
        lax.fori_loop(0, V, one_view, 0, unroll=6)
        for group in est_sends:
            for r in ORDER:
                group[r].sent()
        for group in GROUPS:
            over(along_z_back, beyond(min(group)).start, N * len(group))
            for r in group:
                back_halo[r].start()
                back_far[r].start()
        for r in ORDER:
            pl.when(jnp.logical_not(at_seam(r)))(back_close[r].start)
        for r in ORDER:
            back_own[r].start()
        over(along_z_back, W, R)
        for r in ORDER:

            @pl.when(at_seam(r))
            def _():
                back_halo[r].arrived()
                back[beyond(r), close_p] += got_h[r : r + N]
                back_close[r].start()

        for r in ORDER:
            back_far[r].arrived()
            back[rows_of(r), far_p] += got_x[r : r + N, far_p]
            back_third[r].start()
        for r in ORDER:
            back_close[r].arrived(jnp.logical_not(by_seam(r)))
            back_own[r].arrived(by_seam(r))
            if r in back_behind:
                back_behind[r].arrived()
                back[rows_of(r), close_p] += got_x[r : r + N, close_p] + got_y[r : r + N]
            else:
                back[rows_of(r), close_p] += got_x[r : r + N, close_p]
            back_mate[r].start()
        for r in ORDER:
            back_own[r].arrived(jnp.logical_not(by_seam(r)))
            back_close[r].arrived(by_seam(r))
            back_mate[r].arrived()
            if r in back_direct:
                back_direct[r].arrived()
            for x in range(r, r + N):
                total = back[W + x, W : W + D] + got_x[x, W : W + D] + got_n[x]
                if r in back_direct:
                    total = total + got_y[x]
                updated = ext[W + x, W : W + D] * total / count
                if step < ITERS - 1:
                    ext[W + x, W : W + D] = updated
                else:
                    out[pl.ds(x, D, stride=R)] = updated
            if step < ITERS - 1:
                est_mate[r].start()
                est_own[r].start()
                if r in est_direct:
                    est_direct[r].start()
        for group in back_sends:
            for r in ORDER:
                group[r].sent()
    for copy in views:
        copy.sent()


def solution(mesh):
    nz, nt = mesh.shape["zslab"], mesh.shape["tile"]

    def per_device(estimate, view_data, psf, shifts, extents):
        flat = pl.pallas_call(
            functools.partial(kernel, nz, nt),
            out_shape=pltpu.VMEM((D * R, C), F32),
            in_specs=[pl.BlockSpec(memory_space=pltpu.HBM)] * 5,
            out_specs=pl.BlockSpec(memory_space=pltpu.VMEM),
            scratch_shapes=[
                pltpu.VMEM((D * R, C), F32),
                pltpu.VMEM((V * D, RE, C), F32),
                pltpu.VMEM((RE, DE, C), F32),
                pltpu.VMEM((V, RE * D, C), F32),
                pltpu.VMEM((V, D * R, C), F32),
                pltpu.VMEM((V * D * RE, C), F32),
                pltpu.VMEM((RE, DE, C), F32),
                pltpu.VMEM((R, DE, C), F32),
                pltpu.VMEM((R, D, C), F32),
                pltpu.VMEM((R, D, C), F32),
                pltpu.VMEM((R, D, C), F32),
                pltpu.VMEM((V * D, 3 * DE), BF16),
                pltpu.VMEM((DE, 3 * V * D), BF16),
                pltpu.VMEM((V, R, 3 * RE), BF16),
                pltpu.VMEM((V, RE, 3 * R), BF16),
                pltpu.VMEM((V, 2 * C, 2 * C), BF16),
                pltpu.VMEM((V, 2 * C, 2 * C), BF16),
                pltpu.SMEM((V, 3, TAPS), F32),
                pltpu.SMEM((V,), jnp.int32),
                pltpu.SMEM((2, V), jnp.int32),
                pltpu.SemaphoreType.DMA((SEMS,)),
                pltpu.SemaphoreType.DMA((SEMS,)),
                pltpu.SemaphoreType.DMA((5,)),
            ],
            compiler_params=pltpu.CompilerParams(
                collective_id=0, has_side_effects=True, vmem_limit_bytes=60 * 1024 * 1024
            ),
        )(
            estimate.reshape(D * R, C),
            view_data.reshape(V * D, R, C),
            psf,
            shifts,
            extents.T,
        )
        return flat.reshape(D, R, C)

    placed = (P("zslab", "tile", None), P(None, "zslab", "tile", None), P(), P(), P())
    return jax.shard_map(
        per_device, mesh=mesh, in_specs=placed, out_specs=P("zslab", "tile", None), check_vma=False
    )
```

```python
import functools

import jax
import jax.numpy as jnp
from jax import lax
from jax.experimental import pallas as pl
from jax.experimental.pallas import tpu as pltpu
from jax.sharding import PartitionSpec as P

MESH = pl.DeviceIdType.MESH
V, TAPS, ITERS = 6, 31, 2
H = TAPS // 2
W = 16
D, R, C = 16, 32, 128
DE, RE = D + 2 * W, R + 2 * W
N = 4
ORDER = (0, 28, 4, 24, 8, 20, 12, 16)
GROUPS = ((0, 4), (24, 28), (8, 12), (16, 20))
SIDES = ((0, 4, 8, 12), (16, 20, 24, 28))
DIRECT = 3
SEMS = 2 + 12 * len(ORDER)
F32, BF16 = jnp.float32, jnp.bfloat16


def halves(x):
    hi = x.astype(BF16)
    return hi, (x - hi.astype(F32)).astype(BF16)


def stacked(x):
    hi, lo = halves(x)
    return jnp.concatenate([hi, lo, hi], axis=0)


def dot(a, b):
    return jnp.dot(a, b, preferred_element_type=F32)


def split_part(value):
    hi, lo = halves(value)
    return hi.astype(F32), lo.astype(F32)


def iota(shape, dim):
    return lax.broadcasted_iota(jnp.int32, shape, dim)


def taps(psf, v, a):
    lane = iota((8, C), 1)
    forward = jnp.zeros((8, C), F32)
    reverse = jnp.zeros((8, C), F32)
    for t in range(TAPS):
        p = psf[v, a, t]
        forward = jnp.where(lane == t, p, forward)
        reverse = jnp.where(lane == TAPS - 1 - t, p, reverse)
    weight = jnp.sum(forward, axis=1, keepdims=True)
    return forward / weight, reverse / weight


def slanted(row, rows, first):
    whole = jnp.concatenate([row] * (rows // 8), axis=0)
    return pltpu.roll(whole, first % C, 1, stride=1, stride_axis=0)


def kernel(
    nz, nt, est, view, psf_in, shifts_in, extents_in, out,
    raw, near, ext, zbuf, xbuf, rbuf, back, got_x, got_y, got_n, got_h,
    kz, kzt, kx, kxt, ky, kyt, psf, shifts, extents, send, recv, local,
):
    zs, ti = lax.axis_index("zslab"), lax.axis_index("tile")
    odd = lax.rem(zs, 2)
    mate, ahead, behind = zs + 1 - 2 * odd, zs + 2 - 4 * odd, zs - 2 + 4 * odd
    other = zs - 1 + 2 * odd
    close = pl.multiple_of(2 * W * (1 - odd), W)
    far = pl.multiple_of(2 * W * odd, W)
    is_mate = mate < nz

    class Sent:
        def __init__(self, number, src, dst, target, exists, comes):
            self.exists, self.comes = exists, comes
            self.copy = pltpu.make_async_remote_copy(
                src_ref=src, dst_ref=dst, send_sem=send.at[number], recv_sem=recv.at[number],
                device_id=target, device_id_type=MESH,
            )

        def start(self):
            pl.when(self.exists)(self.copy.start)

        def sent(self):
            pl.when(self.exists)(self.copy.wait_send)

        def arrived(self, where=True):
            pl.when(self.comes & where)(self.copy.wait_recv)

    is_ahead = (ahead >= 0) & (ahead < nz)
    is_behind = (behind >= 0) & (behind < nz)
    is_other = (other >= 0) & (other < nz)
    is_left, is_right = ti > 0, ti < nt - 1
    seam = nt // 2 if nz % 2 == 0 else -1
    seam_left, seam_right = is_left & (ti == seam), is_right & (ti == seam - 1)
    left = {"zslab": jnp.where(seam_left, mate, zs), "tile": ti - 1}
    right = {"zslab": jnp.where(seam_right, mate, zs), "tile": ti + 1}
    numbers = iter(range(SEMS))

    def to_mate(src, dst):
        return Sent(next(numbers), src, dst, {"zslab": mate}, is_mate, is_mate)

    def to_other(src, dst):
        return Sent(next(numbers), src, dst, {"zslab": other}, is_other, is_other)

    def to_ahead(src, dst, where=True):
        return Sent(
            next(numbers), src, dst, {"zslab": ahead}, is_ahead & where, is_behind & where
        )

    def to_behind(src, dst, where=True):
        return Sent(
            next(numbers), src, dst, {"zslab": behind}, is_behind & where, is_ahead & where
        )

    reads = [
        pltpu.make_async_copy(src, dst, local.at[k])
        for k, (src, dst) in enumerate(
            [(est, raw), (view, near.at[:, W : W + R]), (psf_in, psf), (shifts_in, shifts), (extents_in, extents)]
        )
    ]
    for read in reads:
        read.start()

    ext[...] = jnp.zeros(ext.shape, F32)
    got_x[...] = jnp.zeros(got_x.shape, F32)
    got_y[...] = jnp.zeros(got_y.shape, F32)
    got_h[...] = jnp.zeros(got_h.shape, F32)
    near[:, 0:W] = jnp.zeros((V * D, W, C), F32)
    near[:, W + R :] = jnp.zeros((V * D, W, C), F32)
    barrier = pltpu.get_barrier_semaphore()
    beside = [
        ({"zslab": mate}, is_mate), ({"zslab": other}, is_other), ({"zslab": ahead}, is_ahead), ({"zslab": behind}, is_behind),
        ({"tile": ti - 1}, is_left), ({"tile": ti + 1}, is_right),
        (left, seam_left), (right, seam_right),
    ]
    for target, exists in beside:

        @pl.when(exists)
        def _(target=target):
            pl.semaphore_signal(barrier, inc=1, device_id=target, device_id_type=MESH)

    reads[0].wait()
    for x in range(R):
        ext[W + x, W : W + D] = raw[pl.ds(x, D, stride=R)]
    pl.semaphore_wait(barrier, sum(exists.astype(jnp.int32) for _, exists in beside))

    own_p, close_p, far_p = pl.ds(W, D), pl.ds(close, W), pl.ds(far, W)

    def rows_of(r):
        return slice(W + r, W + r + N)

    def beyond(r):
        return slice(W + R + r, W + R + r + N) if r < W else slice(r - W, r - W + N)

    def crossed(where, p):
        if p is far_p:
            return p
        start, other = (W, far) if p is own_p else (close, W)
        return pl.ds(pl.multiple_of(jnp.where(where, other, start), W), W)

    def to_tile(leftward, src, dst, p):
        seam_out, seam_in = (seam_left, seam_right) if leftward else (seam_right, seam_left)
        exists, comes = (is_left, is_right) if leftward else (is_right, is_left)
        if p is far_p:
            exists, comes = exists & jnp.logical_not(seam_out), comes & jnp.logical_not(seam_in)
        return Sent(
            next(numbers), src, dst.at[:, crossed(seam_out, p)], left if leftward else right, exists, comes
        )

    def est_tile(r, p):
        return to_tile(r < W, ext.at[rows_of(r), p], ext.at[beyond(r)], p)

    def back_tile(r, p):
        return to_tile(r >= W, back.at[beyond(r), p], got_x.at[r : r + N], p)

    def at_seam(r):
        return seam_right if r < W else seam_left

    def by_seam(r):
        return seam_left if r < W else seam_right

    views = [
        Sent(next(numbers), view.at[:, 0:W], near.at[:, W + R : RE], {"tile": ti - 1}, is_left, is_right),
        Sent(next(numbers), view.at[:, R - W : R], near.at[:, 0:W], {"tile": ti + 1}, is_right, is_left),
    ]
    est_mate = {r: to_mate(ext.at[rows_of(r), own_p], ext.at[rows_of(r), far_p]) for r in ORDER}
    est_ahead = {
        r: to_ahead(ext.at[rows_of(r), close_p], ext.at[rows_of(r), far_p]) for r in ORDER[:-DIRECT]
    }
    est_direct = {
        r: to_other(ext.at[rows_of(r), own_p], ext.at[rows_of(r), close_p]) for r in ORDER[-DIRECT:]
    }
    est_third = est_ahead | est_direct
    est_halo = {
        r: to_ahead(ext.at[beyond(r), close_p], ext.at[beyond(r), far_p], at_seam(r)) for r in ORDER
    }
    est_own = {r: est_tile(r, own_p) for r in ORDER}
    est_close = {r: est_tile(r, close_p) for r in ORDER}
    est_far = {r: est_tile(r, far_p) for r in ORDER}
    back_halo = {r: to_behind(back.at[beyond(r), far_p], got_h.at[r : r + N], at_seam(r)) for r in ORDER}
    back_far = {r: back_tile(r, far_p) for r in ORDER}
    back_close = {r: back_tile(r, close_p) for r in ORDER}
    back_own = {r: back_tile(r, own_p) for r in ORDER}
    back_behind = {
        r: to_behind(back.at[rows_of(r), far_p], got_y.at[r : r + N]) for r in ORDER[DIRECT:]
    }
    back_direct = {
        r: to_other(back.at[rows_of(r), far_p], got_y.at[r : r + N]) for r in ORDER[:DIRECT]
    }
    back_third = back_behind | back_direct
    back_mate = {r: to_mate(back.at[rows_of(r), close_p], got_n.at[r : r + N]) for r in ORDER}
    est_sends = [est_mate, est_third, est_halo, est_own, est_close, est_far]
    back_sends = [back_halo, back_far, back_close, back_own, back_third, back_mate]

    def build():
        lane = iota((C, C), 1)
        gap = iota((C, C), 0) - lane
        banded = (gap >= -H) & (gap <= H)

        def one(v, total):
            forward, reverse = taps(psf, v, 2)
            hi, lo = split_part(slanted(forward, D, 1))
            low = pltpu.roll(lo, 2 * DE, 1)
            at = pl.ds(pl.multiple_of(v * D, D), D)
            kz[at, 0:C] = (
                hi + pltpu.roll(hi, DE, 1) + jnp.where(lane[0:D] >= 2 * DE, low, 0.0)
            ).astype(BF16)
            kz[at, C:] = low[:, 0 : 3 * DE - C].astype(BF16)
            z_back = jnp.where(lane[0:DE] < D, slanted(reverse, DE, -TAPS), 0.0)
            forward, reverse = taps(psf, v, 0)
            hi, lo = split_part(slanted(forward, R, 1))
            kx[v, :, 0:C] = (hi + pltpu.roll(hi, RE, 1)).astype(BF16)
            kx[v, :, C:] = lo[:, 0:RE].astype(BF16)
            hi, lo = split_part(jnp.where(lane[0:RE] < R, slanted(reverse, RE, -TAPS), 0.0))
            kxt[v] = (hi + pltpu.roll(hi, R, 1) + pltpu.roll(lo, 2 * R, 1))[:, 0 : 3 * R].astype(BF16)
            forward, reverse = taps(psf, v, 1)
            for mat, row in ((ky, reverse), (kyt, forward)):
                hi, lo = halves(jnp.where(banded, slanted(row, C, -H), 0.0))
                mat[v, 0:C, 0:C] = hi
                mat[v, 0:C, C:] = lo
                mat[v, C:, 0:C] = hi
                mat[v, C:, C:] = jnp.zeros((C, C), BF16)
            return total + pltpu.roll(z_back, v * D, 1)

        hi, lo = split_part(lax.fori_loop(0, V, one, jnp.zeros((DE, C), F32)))
        again, low = pltpu.roll(hi, V * D, 1), pltpu.roll(lo, 2 * V * D - C, 1)
        kzt[:, 0:C] = jnp.where(lane[0:DE] < V * D, hi, again).astype(BF16)
        kzt[:, C : 2 * C] = jnp.where(lane[0:DE] < 2 * V * D - C, again, low).astype(BF16)
        kzt[:, 2 * C :] = low[:, 0 : 3 * V * D - 2 * C].astype(BF16)

    def along_z(i, carry):
        x = 2 * i
        o = dot(kz[...], stacked(jnp.concatenate([ext[x], ext[x + 1]], axis=1)))
        for v in range(V):
            for k in range(2):
                at = (x + k) * D
                zbuf[v, pl.ds(at, D)] = o[v * D : (v + 1) * D, k * C : (k + 1) * C]
        return carry

    def one_view(v, carry):
        for i in range(0, D, 2):
            both = [zbuf[v, pl.ds(i + k, RE, stride=D)] for k in range(2)]
            o = dot(kx[v], stacked(jnp.concatenate(both, axis=1)))
            xbuf[v, i * R : (i + 1) * R] = o[:, :C]
            xbuf[v, (i + 1) * R : (i + 2) * R] = o[:, C:]
        o = dot(jnp.concatenate(halves(xbuf[v]), axis=1), ky[v])
        blurred = o[:, :C] + o[:, C:]
        start = W + shifts[v]
        for z in range(D):
            plane = zs * D + z
            inside = jnp.where((plane >= extents[0, v]) & (plane < extents[1, v]), 1.0, 0.0)
            data = near[v * D + z, pl.ds(start, R)]
            xbuf[v, z * R : (z + 1) * R] = inside * data / blurred[z * R : (z + 1) * R]
        o = dot(jnp.concatenate(halves(xbuf[v]), axis=1), kyt[v])
        xbuf[v] = o[:, :C] + o[:, C:]
        for i in range(0, D, 2):
            both = [xbuf[v, (i + k) * R : (i + k + 1) * R] for k in range(2)]
            o = dot(kxt[v], stacked(jnp.concatenate(both, axis=1)))
            for k in range(2):
                at = pl.multiple_of((v * D + i + k) * RE, RE)
                rbuf[pl.ds(at, RE)] = o[:, k * C : (k + 1) * C]
        return carry

    def along_z_back(i, carry):
        x = 2 * i
        both = [rbuf[pl.ds(x + k, V * D, stride=RE)] for k in range(2)]
        o = dot(kzt[...], stacked(jnp.concatenate(both, axis=1)))
        back[x] = o[:, :C]
        back[x + 1] = o[:, C:]
        return carry

    def over(body, first, rows):
        for i in range(first // 2, (first + rows) // 2):
            body(i, 0)

    for r in ORDER:
        est_mate[r].start()
        est_own[r].start()
    for copy in est_direct.values():
        copy.start()
    for copy in views:
        copy.start()
    for read in reads[2:]:
        read.wait()
    build()
    depth = zs * D + iota((D, C), 0)
    count = jnp.zeros((D, C), F32)
    for v in range(V):
        held = (depth >= extents[0, v]) & (depth < extents[1, v])
        count = count + jnp.where(held, 1.0, 0.0)

    for step in range(ITERS):
        for r in ORDER:
            est_mate[r].arrived()
            if r in est_ahead:
                est_ahead[r].start()
            est_close[r].start()
        for r in ORDER:
            est_own[r].arrived(at_seam(r))
            est_halo[r].start()
        for r in ORDER:
            est_third[r].arrived()
            est_far[r].start()
        over(along_z, W, R)
        for side in SIDES:
            for r in side:
                est_own[r].arrived(jnp.logical_not(at_seam(r)))
                est_close[r].arrived()
                est_far[r].arrived()
                est_halo[r].arrived()
            over(along_z, beyond(min(side)).start, N * len(side))
        if step == 0:
            reads[1].wait()
            for copy in views:
                copy.arrived()
        lax.fori_loop(0, V, one_view, 0, unroll=6)
        for group in est_sends:
            for r in ORDER:
                group[r].sent()
        for group in GROUPS:
            over(along_z_back, beyond(min(group)).start, N * len(group))
            for r in group:
                back_halo[r].start()
                back_far[r].start()
        for r in ORDER:
            pl.when(jnp.logical_not(at_seam(r)))(back_close[r].start)
        for r in ORDER:
            back_own[r].start()
        over(along_z_back, W, R)
        for r in ORDER:

            @pl.when(at_seam(r))
            def _():
                back_halo[r].arrived()
                back[beyond(r), close_p] += got_h[r : r + N]
                back_close[r].start()

        for r in ORDER:
            back_far[r].arrived()
            back[rows_of(r), far_p] += got_x[r : r + N, far_p]
            back_third[r].start()
        for r in ORDER:
            back_close[r].arrived(jnp.logical_not(by_seam(r)))
            back_own[r].arrived(by_seam(r))
            if r in back_behind:
                back_behind[r].arrived()
                back[rows_of(r), close_p] += got_x[r : r + N, close_p] + got_y[r : r + N]
            else:
                back[rows_of(r), close_p] += got_x[r : r + N, close_p]
            back_mate[r].start()
        for r in ORDER:
            back_own[r].arrived(jnp.logical_not(by_seam(r)))
            back_close[r].arrived(by_seam(r))
            back_mate[r].arrived()
            if r in back_direct:
                back_direct[r].arrived()
            for x in range(r, r + N):
                total = back[W + x, W : W + D] + got_x[x, W : W + D] + got_n[x]
                if r in back_direct:
                    total = total + got_y[x]
                updated = ext[W + x, W : W + D] * total / count
                if step < ITERS - 1:
                    ext[W + x, W : W + D] = updated
                else:
                    out[pl.ds(x, D, stride=R)] = updated
            if step < ITERS - 1:
                est_mate[r].start()
                est_own[r].start()
                if r in est_direct:
                    est_direct[r].start()
        for group in back_sends:
            for r in ORDER:
                group[r].sent()
    for copy in views:
        copy.sent()


def solution(mesh):
    nz, nt = mesh.shape["zslab"], mesh.shape["tile"]

    def per_device(estimate, view_data, psf, shifts, extents):
        flat = pl.pallas_call(
            functools.partial(kernel, nz, nt),
            out_shape=pltpu.VMEM((D * R, C), F32),
            in_specs=[pl.BlockSpec(memory_space=pltpu.HBM)] * 5,
            out_specs=pl.BlockSpec(memory_space=pltpu.VMEM),
            scratch_shapes=[
                pltpu.VMEM((D * R, C), F32),
                pltpu.VMEM((V * D, RE, C), F32),
                pltpu.VMEM((RE, DE, C), F32),
                pltpu.VMEM((V, RE * D, C), F32),
                pltpu.VMEM((V, D * R, C), F32),
                pltpu.VMEM((V * D * RE, C), F32),
                pltpu.VMEM((RE, DE, C), F32),
                pltpu.VMEM((R, DE, C), F32),
                pltpu.VMEM((R, D, C), F32),
                pltpu.VMEM((R, D, C), F32),
                pltpu.VMEM((R, D, C), F32),
                pltpu.VMEM((V * D, 3 * DE), BF16),
                pltpu.VMEM((DE, 3 * V * D), BF16),
                pltpu.VMEM((V, R, 3 * RE), BF16),
                pltpu.VMEM((V, RE, 3 * R), BF16),
                pltpu.VMEM((V, 2 * C, 2 * C), BF16),
                pltpu.VMEM((V, 2 * C, 2 * C), BF16),
                pltpu.SMEM((V, 3, TAPS), F32),
                pltpu.SMEM((V,), jnp.int32),
                pltpu.SMEM((2, V), jnp.int32),
                pltpu.SemaphoreType.DMA((SEMS,)),
                pltpu.SemaphoreType.DMA((SEMS,)),
                pltpu.SemaphoreType.DMA((5,)),
            ],
            compiler_params=pltpu.CompilerParams(
                collective_id=0, has_side_effects=True, vmem_limit_bytes=60 * 1024 * 1024
            ),
        )(
            estimate.reshape(D * R, C),
            view_data.reshape(V * D, R, C),
            psf,
            shifts,
            extents.T,
        )
        return flat.reshape(D, R, C)

    placed = (P("zslab", "tile", None), P(None, "zslab", "tile", None), P(), P(), P())
    return jax.shard_map(
        per_device, mesh=mesh, in_specs=placed, out_specs=P("zslab", "tile", None), check_vma=False
    )
```
